128 devices in a mesh: row: 8 (over y_hi, z), col: 16 (over y_lo, x, core).
Axes of the slice: x: 4, y: 4 (y_hi: 2, y_lo: 2; y = y_hi * 2 + y_lo), z: 4, core: 2. Of those that a mesh axis runs over, the one named last changes fastest.
Arguments:
- entries: float32 [8192, 8192], P('row', 'col'), may hold values from 0.01 to 1
- pattern: int32 [32, 32], P('row', 'col'), may hold values 0 or 1
- prune: int32 [32, 32], P('row', 'col'), may hold values 0 or 1
Outputs:
- result: float32 [8192, 8192], P('row', 'col')
The draws below stay inside these ranges and needn't reach their ends.
All inputs are finite; a program needn't handle non-finite values. No bound on the sum of `pattern` or of `prune` on one device may be relied on, other than what follows from the above.
Results may differ from the reference program's by a relative error of at most 0.00038.
Values may be sent and summed in bfloat16 or wider, within the bound.
No kernel may reach another device: no remote copies, remote signals or barrier semaphores. Data moves between devices by JAX's collectives and lax.ppermute only.
A program may use at most 128 MiB of HBM per device.

```python
import math
import jax
import jax.numpy as jnp

TILE = 256
GRID = 32
NROWS = 8192


def with_ends(result, rng, least, high):
    dims = result.shape
    place = [jax.random.randint(jax.random.fold_in(rng, axis), (), 0, dims[axis]) for axis in range(len(dims))]
    result = result.at[tuple(place)].set(least)
    longest = dims.index(max(dims))
    place[longest] = (place[longest] + 1) % dims[longest]
    return result.at[tuple(place)].set(high)


def shard_levels(rng, extent, pieces, smallest, top_value):
    def one(dim, parts):
        draws = jax.random.uniform(jax.random.fold_in(jax.random.fold_in(rng, 6), dim), (parts,), jnp.float32, smallest / len(pieces), top_value / len(pieces))
        return jnp.repeat(jnp.exp(draws), extent[dim] // parts).reshape((-1,) + (1,) * (len(extent) - dim - 1))

    loudness = one(*pieces[0])
    for cut in pieces[1:]:
        loudness = loudness * one(*cut)
    return loudness


def setup_inputs(seed: int = 0) -> dict:
    splits = jax.random.split(jax.random.key(seed), 4)
    return {
        "entries": jnp.clip(jnp.exp(math.log(1.0) - 4.6051702 * jax.random.uniform(splits[0], (NROWS, NROWS), jnp.float32) ** shard_levels(splits[0], (NROWS, NROWS), ((0, 8), (1, 16)), -0.2, 0.2)), 0.01, 1.0),
        "pattern": with_ends((jax.random.randint(splits[1], (GRID, GRID), 0, 2) < 1).astype(jnp.int32), jax.random.fold_in(splits[1], 1), 0, 1),
        "prune": with_ends((jax.random.randint(splits[2], (GRID, GRID), 0, 2) < 1).astype(jnp.int32), jax.random.fold_in(splits[2], 1), 0, 1),
    }


def expand_keep(flags):
    count = flags.shape[0]
    diagonal = jnp.eye(count, dtype=jnp.int32)
    keep = jnp.maximum(flags, diagonal).astype(jnp.float32)
    return jnp.repeat(jnp.repeat(keep, TILE, axis=0), TILE, axis=1)


def reference(entries, pattern, prune):
    masked = entries * expand_keep(pattern)
    colsum = jnp.sum(masked, axis=0)
    stoch = (masked / colsum[None, :]).astype(jnp.bfloat16)
    product = jnp.dot(stoch, stoch, preferred_element_type=jnp.float32)
    inflated = product * product * expand_keep(prune)
    total = jnp.sum(inflated, axis=0)
    return NROWS * inflated / total[None, :]
```

```python
import functools
import jax
import jax.numpy as jnp
from jax import lax
from jax.experimental import pallas as pl
from jax.experimental.pallas import tpu as pltpu
from jax.sharding import PartitionSpec as P

AXES = ("row", "col")
YH, NZ, YL, NX, NC = 2, 4, 2, 4, 2
F32 = jnp.float32
BF16 = jnp.bfloat16
I32 = jnp.int32


def place(yh, z, yl, x, c):
    return (yh * NZ + z) * (YL * NX * NC) + (yl * NX + x) * NC + c


def pairs(step):
    return [
        (place(yh, z, yl, x, c), place(*step(yh, z, yl, x, c)))
        for yh in range(YH)
        for z in range(NZ)
        for yl in range(YL)
        for x in range(NX)
        for c in range(NC)
    ]


RING_X = pairs(lambda yh, z, yl, x, c: (yh, z, yl, (x + 1 - 2 * c) % NX, c))
RING_Z = pairs(lambda yh, z, yl, x, c: (yh, (z + 1 - 2 * c) % NZ, yl, x, c))
SWAP_CORE = pairs(lambda yh, z, yl, x, c: (yh, z, yl, x, 1 - c))
SWAP_YL = pairs(lambda yh, z, yl, x, c: (yh, z, 1 - yl, x, c))
SWAP_YH = pairs(lambda yh, z, yl, x, c: (1 - yh, z, yl, x, c))
Z_NEAR = pairs(lambda yh, z, yl, x, c: (yh, z ^ 1, yl, x, c))
Z_FAR = pairs(lambda yh, z, yl, x, c: (yh, 3 - z, yl, x, c))
X_NEAR = pairs(lambda yh, z, yl, x, c: (yh, z, yl, x ^ 1, c))
X_FAR = pairs(lambda yh, z, yl, x, c: (yh, z, yl, 3 - x, c))


def move(value, perm):
    return lax.ppermute(value, AXES, perm)


def add_up(value, perms):
    for perm in perms:
        value = value + move(value, perm)
    return value


def scale_kernel(keep_ref, entries_ref, colsum_ref, out_ref):
    keep = keep_ref[pl.program_id(0), pl.program_id(1)].astype(F32)
    out_ref[0] = (entries_ref[...] * keep / colsum_ref[...]).astype(BF16)


def scaled_tiles(entries, keep, colsum):
    rows, cols = keep.shape
    tall, wide = entries.shape[0] // rows, entries.shape[1] // cols
    return pl.pallas_call(
        scale_kernel,
        grid=(rows, cols),
        out_shape=jax.ShapeDtypeStruct((rows * cols, tall, wide), BF16),
        in_specs=[
            pl.BlockSpec(memory_space=pltpu.SMEM),
            pl.BlockSpec((tall, wide), lambda i, j: (i, j)),
            pl.BlockSpec((1, wide), lambda i, j: (0, j)),
        ],
        out_specs=pl.BlockSpec((1, tall, wide), lambda i, j: (i * cols + j, 0, 0)),
        name="scale",
    )(keep, entries, colsum[None, :])


def product_kernel(n_a, n_b, rows, cols, grid, *refs):
    base_a, base_b, need_a, need_b, count, order = refs[:6]
    a_in = refs[6:6 + n_a]
    b_in = refs[6 + n_a:6 + n_a + n_b]
    out_ref, sum_ref, a_buf, b_buf, acc, a_sem, b_sem = refs[6 + n_a + n_b:]

    def each(act):
        def a_tile(u, t):
            slot = base_a[u] + (t // cols) * grid + t % cols

            @pl.when(need_a[slot] > 0)
            def _():
                act(pltpu.make_async_copy(a_in[u].at[t], a_buf.at[slot], a_sem.at[slot]))

        def b_tile(u, t):
            slot = base_b[u] + t

            @pl.when(need_b[slot] > 0)
            def _():
                act(pltpu.make_async_copy(b_in[u].at[t], b_buf.at[slot], b_sem.at[slot]))

        for u in range(n_a):
            lax.fori_loop(0, rows * cols, lambda t, _, u=u: (a_tile(u, t), 0)[1], 0)
        for u in range(n_b):
            lax.fori_loop(0, rows * cols, lambda t, _, u=u: (b_tile(u, t), 0)[1], 0)

    each(lambda copy: copy.start())
    each(lambda copy: copy.wait())

    tile = acc.shape[0]
    for j in range(cols):
        total = jnp.zeros((1, tile), F32)
        for i in range(rows):
            acc[...] = jnp.zeros_like(acc)

            def step(n, _, i=i, j=j):
                k = order[i * cols + j, n]
                acc[...] += jnp.dot(
                    a_buf[i * grid + k], b_buf[k * cols + j], preferred_element_type=F32
                )
                return 0

            lax.fori_loop(0, count[i * cols + j], step, 0)
            square = acc[...] * acc[...]
            out_ref[i * tile:(i + 1) * tile, j * tile:(j + 1) * tile] = square
            total = total + jnp.sum(square, axis=0, keepdims=True)
        sum_ref[:, j * tile:(j + 1) * tile] = total


def product(a_units, b_units, base_a, base_b, left, right, keep_out):
    rows, cols = keep_out.shape
    grid = left.shape[1]
    tile = a_units[0].shape[1]
    used = left[:, None, :] * right.T[None, :, :] * keep_out[:, :, None]
    need_a = jnp.max(used, axis=1).reshape(-1)
    need_b = jnp.max(used, axis=0).T.reshape(-1)
    used = used.reshape(rows * cols, grid)
    count = jnp.sum(used, axis=1)
    rank = jnp.cumsum(used, axis=1) - 1
    ids = jnp.arange(grid, dtype=I32)
    hit = (rank[:, :, None] == ids[None, None, :]) & (used[:, :, None] > 0)
    order = jnp.sum(jnp.where(hit, ids[None, :, None], 0), axis=1)
    smem = pl.BlockSpec(memory_space=pltpu.SMEM)
    return pl.pallas_call(
        functools.partial(product_kernel, len(a_units), len(b_units), rows, cols, grid),
        out_shape=(
            jax.ShapeDtypeStruct((rows * tile, cols * tile), F32),
            jax.ShapeDtypeStruct((1, cols * tile), F32),
        ),
        in_specs=[smem] * 6 + [pl.BlockSpec(memory_space=pl.ANY)] * (len(a_units) + len(b_units)),
        out_specs=(
            pl.BlockSpec(memory_space=pltpu.VMEM),
            pl.BlockSpec(memory_space=pltpu.VMEM),
        ),
        scratch_shapes=[
            pltpu.VMEM((rows * grid, tile, tile), BF16),
            pltpu.VMEM((cols * grid, tile, tile), BF16),
            pltpu.VMEM((tile, tile), F32),
            pltpu.SemaphoreType.DMA((rows * grid,)),
            pltpu.SemaphoreType.DMA((cols * grid,)),
        ],
        compiler_params=pltpu.CompilerParams(vmem_limit_bytes=40 * 1024 * 1024),
        name="product",
    )(base_a, base_b, need_a, need_b, count, order, *a_units, *b_units)


def tile_keep(flags):
    tile_rows, tile_cols = flags.shape
    row_ids = lax.axis_index("row") * tile_rows + jnp.arange(tile_rows, dtype=I32)
    col_ids = lax.axis_index("col") * tile_cols + jnp.arange(tile_cols, dtype=I32)
    diagonal = (row_ids[:, None] == col_ids[None, :]).astype(I32)
    return jnp.maximum(flags, diagonal)


def shards(entries, pattern, prune):
    row, col = lax.axis_index("row"), lax.axis_index("col")
    rows, cols = pattern.shape
    height, width = entries.shape
    grid = rows * lax.axis_size("row")
    yh, z = row // NZ, row % NZ
    yl, x, c = col // (NX * NC), (col // NC) % NX, col % NC

    keep = tile_keep(pattern)
    keep_out = tile_keep(prune)
    keep_f = keep.astype(F32)
    masked = (
        entries.reshape(rows, height // rows, cols, width // cols) * keep_f[:, None, :, None]
    ).reshape(height, width)

    flags = lax.dynamic_update_slice(jnp.zeros((grid, cols), F32), keep_f, (row * rows, 0))
    sums = jnp.concatenate([jnp.sum(masked, axis=0), flags.reshape(-1)])
    sums = add_up(sums, (Z_NEAR, Z_FAR, SWAP_YH))
    colsum = sums[:width]
    right = sums[width:].reshape(grid, cols).astype(I32)

    own = scaled_tiles(entries, keep, colsum)

    left = lax.dynamic_update_slice(jnp.zeros((rows, grid), F32), keep_f, (0, col * cols))
    left = add_up(left.reshape(-1), (SWAP_CORE, SWAP_YL, X_NEAR, X_FAR)).reshape(rows, grid).astype(I32)

    other = move(own, SWAP_CORE)
    xa = move(own, RING_X)
    za = move(own, RING_Z)
    px = move(own, SWAP_YL)
    pz = move(own, SWAP_YH)
    xb = move(other, RING_X)
    zb = move(other, RING_Z)
    xc = move(xa, RING_X)
    zc = move(za, RING_Z)
    px_o = move(px, SWAP_CORE)
    pz_o = move(pz, SWAP_CORE)
    pxa = move(px, RING_X)
    pxb = move(px_o, RING_X)
    pxc = move(pxa, RING_X)
    pza = move(pz, RING_Z)
    pzb = move(pz_o, RING_Z)
    pzc = move(pza, RING_Z)
    swap = lambda v: move(v, SWAP_CORE)

    near, back = (x - 1 + 2 * c) % NX, (x + 1 - 2 * c) % NX
    far = (x + 2) % NX
    a_units, base_a = [], []

    def a_unit(value, yl_of, x_of, core_of):
        a_units.append(value)
        base_a.append(((yl_of * NX + x_of) * NC + core_of) * cols)

    d = 1 - c
    for y, (u0, u1), (ua, ub, uc) in (
        (yl, (own, other), (xa, xb, xc)),
        (1 - yl, (px, px_o), (pxa, pxb, pxc)),
    ):
        a_unit(u0, y, x, c)
        a_unit(u1, y, x, d)
        a_unit(ua, y, near, c)
        a_unit(ub, y, near, d)
        a_unit(swap(ua), y, back, d)
        a_unit(swap(ub), y, back, c)
        a_unit(uc, y, far, c)
        a_unit(swap(uc), y, far, d)

    near, back = (z - 1 + 2 * c) % NZ, (z + 1 - 2 * c) % NZ
    far = (z + 2) % NZ
    b_units, base_b = [], []

    def b_unit(value, yh_of, z_of):
        b_units.append(value)
        base_b.append((yh_of * NZ + z_of) * rows * cols)

    for y, u0, (ua, ub, uc) in ((yh, own, (za, zb, zc)), (1 - yh, pz, (pza, pzb, pzc))):
        b_unit(u0, y, z)
        b_unit(ua, y, near)
        b_unit(swap(ub), y, back)
        b_unit(uc, y, far)

    inflated, total = product(
        a_units, b_units, jnp.stack(base_a).astype(I32), jnp.stack(base_b).astype(I32), left, right, keep_out
    )
    total = add_up(total[0], (Z_NEAR, Z_FAR, SWAP_YH))
    order = float(height * lax.axis_size("row"))
    return order * inflated / total[None, :]


def solution(mesh):
    return jax.shard_map(
        shards,
        mesh=mesh,
        in_specs=(P("row", "col"), P("row", "col"), P("row", "col")),
        out_specs=P("row", "col"),
        check_vma=False,
    )
```

```python
import functools
import jax
import jax.numpy as jnp
from jax import lax
from jax.experimental import pallas as pl
from jax.experimental.pallas import tpu as pltpu
from jax.sharding import PartitionSpec as P

AXES = ("row", "col")
YH, NZ, YL, NX, NC = 2, 4, 2, 4, 2
F32 = jnp.float32
BF16 = jnp.bfloat16
I32 = jnp.int32
GROUP = 4


def place(yh, z, yl, x, c):
    return (yh * NZ + z) * (YL * NX * NC) + (yl * NX + x) * NC + c


def pairs(step):
    return [
        (place(yh, z, yl, x, c), place(*step(yh, z, yl, x, c)))
        for yh in range(YH)
        for z in range(NZ)
        for yl in range(YL)
        for x in range(NX)
        for c in range(NC)
    ]


X_UP = pairs(lambda yh, z, yl, x, c: (yh, z, yl, (x + 1) % NX, c))
X_DOWN = pairs(lambda yh, z, yl, x, c: (yh, z, yl, (x - 1) % NX, c))
Z_UP = pairs(lambda yh, z, yl, x, c: (yh, (z + 1) % NZ, yl, x, c))
Z_DOWN = pairs(lambda yh, z, yl, x, c: (yh, (z - 1) % NZ, yl, x, c))
SWAP_CORE = pairs(lambda yh, z, yl, x, c: (yh, z, yl, x, 1 - c))
SWAP_YL = pairs(lambda yh, z, yl, x, c: (yh, z, 1 - yl, x, c))
SWAP_YH = pairs(lambda yh, z, yl, x, c: (1 - yh, z, yl, x, c))
Z_TURNS = [pairs(lambda yh, z, yl, x, c, d=d: (yh, (z + d) % NZ, yl, x, c)) for d in range(1, NZ)]
X_TURNS = [pairs(lambda yh, z, yl, x, c, d=d: (yh, z, yl, (x + d) % NX, c)) for d in range(1, NX)]


def move(value, perm):
    return lax.ppermute(value, AXES, perm)


def turn_sum(value, turns):
    return value + sum(move(value, turn) for turn in turns)


def row_sum(value):
    value = turn_sum(value, Z_TURNS)
    return value + move(value, SWAP_YH)


def after(value, *deps):
    return lax.optimization_barrier((value, *deps))[0]


def product_kernel(n_a, n_b, shape, cols_out, begun, *refs):
    rows, cols, grid, tile = shape
    base_a, base_b, todo_a, todo_b, n_todo_a, n_todo_b, count, order = refs[:8]
    refs = refs[8:]
    if begun:
        start_ref, refs = refs[0], refs[1:]
    a_in, b_in, refs = refs[:n_a], refs[n_a:n_a + n_b], refs[n_a + n_b:]
    out_ref, a_buf, b_buf, acc, a_sem, b_sem = refs
    no_a, no_b = rows * grid, cols * grid
    deep = a_in[0].shape[1] // tile

    def tile_at(ref, i, j):
        return ref.at[pl.ds(pl.multiple_of(i * tile, tile), tile), pl.ds(pl.multiple_of(j * tile, tile), tile)]

    def each(act):
        for u in range(n_a):
            def a_tile(n, _, u=u):
                t = todo_a[u, n]
                i, j = t // deep, t % deep
                slot = base_a[u] + i * grid + j
                act(pltpu.make_async_copy(tile_at(a_in[u], i, j), a_buf.at[slot], a_sem.at[slot]))
                return 0

            lax.fori_loop(0, n_todo_a[u], a_tile, 0)
        for u in range(n_b):
            def b_tile(n, _, u=u):
                t = todo_b[u, n]
                slot = base_b[u] * cols + t
                act(pltpu.make_async_copy(tile_at(b_in[u], t // cols, t % cols), b_buf.at[slot], b_sem.at[slot]))
                return 0

            lax.fori_loop(0, n_todo_b[u], b_tile, 0)

    each(lambda copy: copy.start())
    a_buf[no_a] = jnp.zeros((tile, tile), BF16)
    b_buf[no_b] = jnp.zeros((tile, tile), BF16)
    each(lambda copy: copy.wait())

    for n_out, j in enumerate(cols_out):
        for i in range(rows):
            down = slice(i * tile, (i + 1) * tile)
            if begun:
                acc[...] = start_ref[down, j * tile:(j + 1) * tile]
            else:
                acc[...] = jnp.zeros_like(acc)

            def step(n, _, i=i, j=j):
                part = None
                for g in range(GROUP):
                    k = order[i * cols + j, n * GROUP + g]
                    a_tile = a_buf[jnp.where(k < grid, i * grid + k, no_a)]
                    b_tile = b_buf[jnp.where(k < grid, k * cols + j, no_b)]
                    dot = jnp.dot(a_tile, b_tile, preferred_element_type=F32)
                    part = dot if part is None else part + dot
                acc[...] += part
                return 0

            lax.fori_loop(0, (count[i * cols + j] + GROUP - 1) // GROUP, step, 0)
            out_ref[down, n_out * tile:(n_out + 1) * tile] = acc[...]


def listed(flags):
    size = flags.shape[1]
    ids = jnp.arange(size, dtype=I32)
    count = jnp.sum(flags, axis=1)
    rank = jnp.cumsum(flags, axis=1) - 1
    hit = (rank[:, :, None] == ids[None, None, :]) & (flags[:, :, None] > 0)
    order = jnp.sum(jnp.where(hit, ids[None, :, None], 0), axis=1)
    return jnp.where(ids[None, :] < count[:, None], order, size).astype(I32), count.astype(I32)


def product(a_units, b_units, used, cols_out, start=None):
    rows, cols, grid = used.shape
    begun = start is not None
    tile = a_units[0][0].shape[0] // rows
    deep = a_units[0][0].shape[1] // tile
    wanted = jnp.stack([used[:, j] if j in cols_out else jnp.zeros_like(used[:, j]) for j in range(cols)], axis=1)
    need_a = jnp.max(wanted, axis=1)
    need_b = jnp.max(wanted, axis=0).T
    base_a = jnp.stack([base for _, base in a_units]).astype(I32)
    base_b = jnp.stack([base for _, base in b_units]).astype(I32)
    todo_a, n_todo_a = listed(
        jnp.stack([lax.dynamic_slice(need_a, (0, base), (rows, deep)).reshape(-1) for _, base in a_units])
    )
    todo_b, n_todo_b = listed(
        jnp.stack([lax.dynamic_slice(need_b, (base, 0), (deep, cols)).reshape(-1) for _, base in b_units])
    )
    order, count = listed(wanted.reshape(rows * cols, grid))
    order = jnp.pad(order, ((0, 0), (0, GROUP - 1)), constant_values=grid)
    smem = pl.BlockSpec(memory_space=pltpu.SMEM)
    vmem = pl.BlockSpec(memory_space=pltpu.VMEM)
    return pl.pallas_call(
        functools.partial(product_kernel, len(a_units), len(b_units), (rows, cols, grid, tile), cols_out, begun),
        out_shape=jax.ShapeDtypeStruct((rows * tile, len(cols_out) * tile), F32),
        in_specs=[smem] * 8
        + [vmem] * begun
        + [pl.BlockSpec(memory_space=pl.ANY)] * (len(a_units) + len(b_units)),
        out_specs=vmem,
        scratch_shapes=[
            pltpu.VMEM((rows * grid + 1, tile, tile), BF16),
            pltpu.VMEM((cols * grid + 1, tile, tile), BF16),
            pltpu.VMEM((tile, tile), F32),
            pltpu.SemaphoreType.DMA((rows * grid,)),
            pltpu.SemaphoreType.DMA((cols * grid,)),
        ],
        compiler_params=pltpu.CompilerParams(vmem_limit_bytes=40 * 1024 * 1024),
        cost_estimate=pl.CostEstimate(flops=4 * 10**9, bytes_accessed=16 * 2**20, transcendentals=0),
        name="finish" if begun else "begin",
    )(
        base_a, base_b, todo_a, todo_b, n_todo_a, n_todo_b, count, order,
        *([start] if begun else []),
        *[value for value, _ in a_units],
        *[value for value, _ in b_units],
    )


def tile_keep(flags):
    tile_rows, tile_cols = flags.shape
    row_ids = lax.axis_index("row") * tile_rows + jnp.arange(tile_rows, dtype=I32)
    col_ids = lax.axis_index("col") * tile_cols + jnp.arange(tile_cols, dtype=I32)
    diagonal = (row_ids[:, None] == col_ids[None, :]).astype(I32)
    return jnp.maximum(flags, diagonal)


def shards(entries, pattern, prune):
    row, col = lax.axis_index("row"), lax.axis_index("col")
    rows, cols = pattern.shape
    height, width = entries.shape
    grid = rows * lax.axis_size("row")
    yh, z = row // NZ, row % NZ
    yl, x, c = col // (NX * NC), (col // NC) % NX, col % NC

    keep = tile_keep(pattern)
    keep_out = tile_keep(prune)
    keep_f = keep.astype(F32)
    masked = (
        entries.reshape(rows, height // rows, cols, width // cols) * keep_f[:, None, :, None]
    ).reshape(height, width)

    left = lax.dynamic_update_slice(jnp.zeros((rows, grid), F32), keep_f, (0, col * cols)).reshape(-1)
    left = turn_sum(left, X_TURNS)
    left = left + move(left, SWAP_YL)

    flags = lax.dynamic_update_slice(jnp.zeros((grid, cols), F32), keep_f, (row * rows, 0))
    sums = jnp.concatenate([jnp.sum(masked, axis=0), flags.reshape(-1)])
    sums = row_sum(sums)
    colsum, right = sums[:width], sums[width:]
    a = (masked / colsum[None, :]).astype(BF16)
    a, left = lax.optimization_barrier((a, left))

    half = height // 2
    mine = lax.dynamic_slice(a, (c * half, 0), (half, width))
    theirs = lax.dynamic_slice(a, ((1 - c) * half, 0), (half, width))
    b = jnp.concatenate([mine, move(theirs, SWAP_CORE)], axis=1)
    notes = jnp.concatenate([left, right, keep_out.astype(F32).reshape(-1)])
    notes_o = move(notes, SWAP_CORE)

    xl, xr, pa = move(a, X_UP), move(a, X_DOWN), move(a, SWAP_YL)
    zl, zr = move(b, Z_UP), move(b, Z_DOWN)
    a, b, xl, xr, pa, zl, zr = lax.optimization_barrier((a, b, xl, xr, pa, zl, zr))
    pxl, pxr = move(pa, X_UP), move(pa, X_DOWN)
    zf, pb = move(zl, Z_UP), move(b, SWAP_YH)
    a, b, xl, xr, pa, zl, zr, pxl, pxr, zf, pb, notes_o, left, right = lax.optimization_barrier(
        (a, b, xl, xr, pa, zl, zr, pxl, pxr, zf, pb, notes_o, left, right)
    )
    xf, pxf = move(xl, X_UP), move(pxr, X_DOWN)
    pzl, pzr, pzf = move(pb, Z_UP), move(pb, Z_DOWN), move(zf, SWAP_YH)

    n_left, n_right = rows * grid, grid * cols
    left = (left + notes_o[:n_left]).reshape(rows, -1, NC, cols)
    left = lax.dynamic_index_in_dim(left, c, 2, False).reshape(rows, -1)
    right = jnp.concatenate(
        [right.reshape(grid, cols), notes_o[n_left:n_left + n_right].reshape(grid, cols)], axis=1
    )
    right = lax.dynamic_index_in_dim(right.reshape(-1, NC, cols, NC * cols), c, 1, False).reshape(-1, NC * cols)
    out = jnp.concatenate([keep_out.astype(F32), notes_o[n_left + n_right:].reshape(rows, cols)], axis=1)
    used = (left[:, None, :] * right.T[None, :, :] * out[:, :, None]).astype(I32)

    a_unit = lambda value, y, dx: (value, (y * NX + (x + dx) % NX) * cols)
    b_unit = lambda value, y, dz: (value, (y * NZ + (z + dz) % NZ) * cols)
    py, ph = 1 - yl, 1 - yh
    a_early = [
        a_unit(a, yl, 0), a_unit(xl, yl, NX - 1), a_unit(xr, yl, 1),
        a_unit(pa, py, 0), a_unit(pxl, py, NX - 1), a_unit(pxr, py, 1),
    ]
    a_late = [a_unit(xf, yl, 2), a_unit(pxf, py, 2)]
    b_early = [
        b_unit(b, yh, 0), b_unit(zl, yh, NZ - 1), b_unit(zr, yh, 1), b_unit(zf, yh, 2), b_unit(pb, ph, 0),
    ]
    b_late = [b_unit(pzl, ph, NZ - 1), b_unit(pzr, ph, 1), b_unit(pzf, ph, 2)]

    ids = jnp.arange(used.shape[2], dtype=I32)
    late = functools.reduce(
        jnp.logical_or, [(ids >= base) & (ids < base + cols) for _, base in a_late + b_late]
    ).astype(I32)[None, None, :]
    own_cols, other_cols = tuple(range(cols)), tuple(range(cols, NC * cols))
    begun = product(a_early, b_early, used * (1 - late), own_cols + other_cols)
    a_units, b_units, used = a_early + a_late, b_early + b_late, used * late
    part_o = product(a_units, b_units, used, other_cols, begun)
    got = move(part_o, SWAP_CORE)
    part = product(a_units, b_units, used, own_cols, begun)
    full = part + got
    inflated = full * full
    total = row_sum(jnp.sum(inflated, axis=0))
    order = float(height * lax.axis_size("row"))
    return inflated * (order / total)[None, :]


def solution(mesh):
    return jax.shard_map(
        shards,
        mesh=mesh,
        in_specs=(P("row", "col"), P("row", "col"), P("row", "col")),
        out_specs=P("row", "col"),
        check_vma=False,
    )
```

```python
import functools
import jax
import jax.numpy as jnp
from jax import lax
from jax.experimental import pallas as pl
from jax.experimental.pallas import tpu as pltpu
from jax.sharding import PartitionSpec as P

AXES = ("row", "col")
YH, NZ, YL, NX, NC = 2, 4, 2, 4, 2
F32 = jnp.float32
BF16 = jnp.bfloat16
I32 = jnp.int32
GROUP = 2


def place(yh, z, yl, x, c):
    return (yh * NZ + z) * (YL * NX * NC) + (yl * NX + x) * NC + c


def pairs(step):
    return [
        (place(yh, z, yl, x, c), place(*step(yh, z, yl, x, c)))
        for yh in range(YH)
        for z in range(NZ)
        for yl in range(YL)
        for x in range(NX)
        for c in range(NC)
    ]


X_UP = pairs(lambda yh, z, yl, x, c: (yh, z, yl, (x + 1) % NX, c))
X_DOWN = pairs(lambda yh, z, yl, x, c: (yh, z, yl, (x - 1) % NX, c))
Z_UP = pairs(lambda yh, z, yl, x, c: (yh, (z + 1) % NZ, yl, x, c))
Z_DOWN = pairs(lambda yh, z, yl, x, c: (yh, (z - 1) % NZ, yl, x, c))
SWAP_CORE = pairs(lambda yh, z, yl, x, c: (yh, z, yl, x, 1 - c))
SWAP_YL = pairs(lambda yh, z, yl, x, c: (yh, z, 1 - yl, x, c))
SWAP_YH = pairs(lambda yh, z, yl, x, c: (1 - yh, z, yl, x, c))
Z_TURNS = [pairs(lambda yh, z, yl, x, c, d=d: (yh, (z + d) % NZ, yl, x, c)) for d in range(1, NZ)]
X_TURNS = [pairs(lambda yh, z, yl, x, c, d=d: (yh, z, yl, (x + d) % NX, c)) for d in range(1, NX)]


def move(value, perm):
    return lax.ppermute(value, AXES, perm)


def turn_sum(value, turns):
    return value + sum(move(value, turn) for turn in turns)


def row_sum(value):
    value = turn_sum(value, Z_TURNS)
    return value + move(value, SWAP_YH)


def after(value, *deps):
    return lax.optimization_barrier((value, *deps))[0]


def vmem_limit(mib):
    return pltpu.CompilerParams(vmem_limit_bytes=mib * 2**20)


VMEM = pl.BlockSpec(memory_space=pltpu.VMEM)
SMEM = pl.BlockSpec(memory_space=pltpu.SMEM)
ANY = pl.BlockSpec(memory_space=pl.ANY)


def mask_kernel(keep_ref, entries_ref, masked_ref, sum_ref):
    rows, cols = keep_ref.shape
    tall, wide = entries_ref.shape[0] // rows, entries_ref.shape[1] // cols
    for j in range(cols):
        right = slice(j * wide, (j + 1) * wide)
        total = jnp.zeros((1, wide), F32)
        for i in range(rows):
            down = slice(i * tall, (i + 1) * tall)
            masked = entries_ref[down, right] * keep_ref[i, j].astype(F32)
            masked_ref[down, right] = masked
            total = total + jnp.sum(masked, axis=0, keepdims=True)
        sum_ref[:, right] = total


def mask(keep, entries):
    return pl.pallas_call(
        mask_kernel,
        out_shape=(
            jax.ShapeDtypeStruct(entries.shape, F32),
            jax.ShapeDtypeStruct((1, entries.shape[1]), F32),
        ),
        in_specs=[SMEM, VMEM],
        out_specs=(VMEM, VMEM),
        compiler_params=vmem_limit(16),
        name="mask",
    )(keep, entries)


def square_kernel(mine_ref, got_ref, out_ref, sum_ref):
    rows = out_ref.shape[0]
    step = rows // 4
    total = jnp.zeros(sum_ref.shape, F32)
    for r in range(0, rows, step):
        full = mine_ref[r:r + step, :] + got_ref[r:r + step, :]
        square = full * full
        out_ref[r:r + step, :] = square
        total = total + jnp.sum(square, axis=0, keepdims=True)
    sum_ref[...] = total


def squared(mine, got):
    return pl.pallas_call(
        square_kernel,
        out_shape=(
            jax.ShapeDtypeStruct(mine.shape, F32),
            jax.ShapeDtypeStruct((1, mine.shape[1]), F32),
        ),
        in_specs=[VMEM, VMEM],
        out_specs=(VMEM, VMEM),
        compiler_params=vmem_limit(16),
        name="square",
    )(mine, got)


def rescale_kernel(order, value_ref, total_ref, out_ref):
    factor = order / total_ref[...]
    rows = out_ref.shape[0]
    step = rows // 4
    for r in range(0, rows, step):
        out_ref[r:r + step, :] = value_ref[r:r + step, :] * factor


def rescaled(order, value, total):
    return pl.pallas_call(
        functools.partial(rescale_kernel, order),
        out_shape=jax.ShapeDtypeStruct(value.shape, F32),
        in_specs=[VMEM, VMEM],
        out_specs=VMEM,
        compiler_params=vmem_limit(16),
        name="rescale",
    )(value, total)


PLAN_LEFT, PLAN_RIGHT, PLAN_OUT, PLAN_LATE, PLAN_A, PLAN_B, PLAN_SIZE = 0, 4, 8, 24, 25, 33, 48
A_PLACES = [(0, 0), (0, NX - 1), (0, 1), (1, 0), (1, NX - 1), (1, 1), (0, 2), (1, 2)]
B_PLACES = [(0, 0), (0, NZ - 1), (0, 1), (0, 2), (1, 0), (1, NZ - 1), (1, 1), (1, 2)]
A_LATE, B_LATE = (6, 7), (5, 6, 7)


def plan_kernel(rows, cols, left_ref, right_ref, out_ref, other_ref, plan_ref):
    row, col = lax.axis_index("row"), lax.axis_index("col")
    yh, z = row // NZ, row % NZ
    yl, x, c = col // (NX * NC), (col // NC) % NX, col % NC
    parts = YL * NX
    grid = parts * NC * cols
    n_left, n_right = rows * grid, grid * cols

    for i in range(rows):
        def add(q, m, i=i):
            for j in range(cols):
                at = i * grid + (q * NC + c) * cols + j
                flag = ((left_ref[at] + other_ref[at]) > 0.5).astype(I32)
                m = m + flag * (1 << (q * cols + j))
            return m

        plan_ref[PLAN_LEFT + i] = functools.reduce(lambda m, q: add(q, m), range(parts), jnp.int32(0))
    for j in range(NC * cols):
        m = jnp.int32(0)
        for q in range(parts):
            for i in range(cols):
                at = ((q * NC + c) * cols + i) * cols + j % cols
                flag = right_ref[at] if j < cols else other_ref[n_left + at]
                m = m + (flag > 0.5).astype(I32) * (1 << (q * cols + i))
        plan_ref[PLAN_RIGHT + j] = m
    for i in range(rows):
        for j in range(NC * cols):
            if j < cols:
                flag = out_ref[i * cols + j]
            else:
                flag = other_ref[n_left + n_right + i * cols + j - cols]
            plan_ref[PLAN_OUT + i * NC * cols + j] = (flag > 0.5).astype(I32)
    late = jnp.int32(0)
    whole = (1 << cols) - 1
    for u, (dy, dx) in enumerate(A_PLACES):
        base = ((yl + dy) % YL * NX + (x + dx) % NX) * cols
        plan_ref[PLAN_A + u] = base
        if u in A_LATE:
            late = late | lax.shift_left(jnp.int32(whole), base)
    for u, (dy, dz) in enumerate(B_PLACES):
        base = ((yh + dy) % YH * NZ + (z + dz) % NZ) * cols
        plan_ref[PLAN_B + u] = base
        if u in B_LATE:
            late = late | lax.shift_left(jnp.int32(whole), base)
    plan_ref[PLAN_LATE] = late


def planned(rows, cols, left, right, keep_out, other):
    return pl.pallas_call(
        functools.partial(plan_kernel, rows, cols),
        out_shape=jax.ShapeDtypeStruct((PLAN_SIZE,), I32),
        in_specs=[SMEM] * 4,
        out_specs=SMEM,
        name="plan",
    )(left, right, keep_out, other)


def product_kernel(n_a, n_b, shape, cols_out, begun, *refs):
    rows, cols, grid, tile = shape
    plan, refs = refs[0], refs[1:]
    if begun:
        start_ref, refs = refs[0], refs[1:]
    a_in, b_in, refs = refs[:n_a], refs[n_a:n_a + n_b], refs[n_a + n_b:]
    n_out = 1 if begun else 2
    out_refs, (a_buf, b_buf, acc, order, a_sem, b_sem) = refs[:n_out], refs[n_out:]
    wide = len(cols_out)
    no_a, no_b = rows * grid, wide * grid
    deep = a_in[0].shape[1] // tile

    when = plan[PLAN_LATE] if begun else ~plan[PLAN_LATE]
    used = {}
    for i in range(rows):
        for j in cols_out:
            pair = plan[PLAN_LEFT + i] & plan[PLAN_RIGHT + j] & when
            used[i, j] = jnp.where(plan[PLAN_OUT + i * cols + j] > 0, pair, 0)
    need_a = [functools.reduce(jnp.bitwise_or, [used[i, j] for j in cols_out]) for i in range(rows)]
    need_b = [functools.reduce(jnp.bitwise_or, [used[i, j] for i in range(rows)]) for j in cols_out]

    def tile_at(ref, i, j):
        return ref.at[pl.ds(i * tile, tile), pl.ds(j * tile, tile)]

    def each(act):
        for u in range(n_a):
            base = plan[PLAN_A + u]
            for i in range(rows):
                bits = lax.shift_right_logical(need_a[i], base)
                for k in range(deep):
                    @pl.when(bits & (1 << k) > 0)
                    def _(u=u, i=i, k=k, base=base):
                        slot = i * grid + base + k
                        act(pltpu.make_async_copy(tile_at(a_in[u], i, k), a_buf.at[slot], a_sem.at[slot]))
        for u in range(n_b):
            base = plan[PLAN_B + u]
            for n, j in enumerate(cols_out):
                bits = lax.shift_right_logical(need_b[n], base)
                for k in range(deep):
                    @pl.when(bits & (1 << k) > 0)
                    def _(u=u, n=n, j=j, k=k, base=base):
                        slot = n * grid + base + k
                        act(pltpu.make_async_copy(tile_at(b_in[u], k, j), b_buf.at[slot], b_sem.at[slot]))

    each(lambda copy: copy.start())
    a_buf[no_a] = jnp.zeros((tile, tile), BF16)
    b_buf[no_b] = jnp.zeros((tile, tile), BF16)
    count = {}
    for n, j in enumerate(cols_out):
        for i in range(rows):
            first = (n * rows + i) * (grid + GROUP)
            at = jnp.int32(first)
            for k in range(grid):
                order[at] = k
                at = at + (lax.shift_right_logical(used[i, j], k) & 1)
            for g in range(GROUP - 1):
                order[at + g] = grid
            count[i, j] = (at - first + GROUP - 1) // GROUP
    each(lambda copy: copy.wait())

    for n, j in enumerate(cols_out):
        out_ref = out_refs[n * n_out // wide]
        place = n % (wide // n_out)
        for i in range(rows):
            here = slice(i * tile, (i + 1) * tile), slice(place * tile, (place + 1) * tile)
            acc[...] = start_ref[here] if begun else jnp.zeros_like(acc)

            def step(m, _, i=i, n=n):
                part = None
                for g in range(GROUP):
                    k = order[(n * rows + i) * (grid + GROUP) + m * GROUP + g]
                    a_tile = a_buf[jnp.where(k < grid, i * grid + k, no_a)]
                    b_tile = b_buf[jnp.where(k < grid, n * grid + k, no_b)]
                    dot = jnp.dot(a_tile, b_tile, preferred_element_type=F32)
                    part = dot if part is None else part + dot
                acc[...] += part
                return 0

            lax.fori_loop(0, count[i, j], step, 0)
            out_ref[here] = acc[...]


def product(plan, a_units, b_units, rows, cols, cols_out, start=None):
    begun = start is not None
    tile = a_units[0].shape[0] // rows
    grid = YL * NX * (a_units[0].shape[1] // tile)
    half = jax.ShapeDtypeStruct((rows * tile, cols // NC * tile), F32)
    n_out = 1 if begun else NC
    return pl.pallas_call(
        functools.partial(product_kernel, len(a_units), len(b_units), (rows, cols, grid, tile), cols_out, begun),
        out_shape=(half,) * n_out,
        in_specs=[SMEM] + [VMEM] * begun + [ANY] * (len(a_units) + len(b_units)),
        out_specs=(VMEM,) * n_out,
        scratch_shapes=[
            pltpu.VMEM((rows * grid + 1, tile, tile), BF16),
            pltpu.VMEM((len(cols_out) * grid + 1, tile, tile), BF16),
            pltpu.VMEM((tile, tile), F32),
            pltpu.SMEM((rows * len(cols_out) * (grid + GROUP),), I32),
            pltpu.SemaphoreType.DMA((rows * grid,)),
            pltpu.SemaphoreType.DMA((len(cols_out) * grid,)),
        ],
        compiler_params=vmem_limit(26),
        cost_estimate=pl.CostEstimate(flops=10**6, bytes_accessed=2**10, transcendentals=0),
        name="finish" if begun else "begin",
    )(plan, *([start] if begun else []), *a_units, *b_units)


def tile_keep(flags):
    tile_rows, tile_cols = flags.shape
    row_ids = lax.axis_index("row") * tile_rows + jnp.arange(tile_rows, dtype=I32)
    col_ids = lax.axis_index("col") * tile_cols + jnp.arange(tile_cols, dtype=I32)
    diagonal = (row_ids[:, None] == col_ids[None, :]).astype(I32)
    return jnp.maximum(flags, diagonal)


def shards(entries, pattern, prune):
    row, col = lax.axis_index("row"), lax.axis_index("col")
    rows, cols = pattern.shape
    height, width = entries.shape
    grid = rows * lax.axis_size("row")
    c = col % NC

    keep = tile_keep(pattern)
    keep_out = tile_keep(prune)
    keep_f = keep.astype(F32)
    masked, sums = mask(keep, entries)

    left = lax.dynamic_update_slice(jnp.zeros((rows, grid), F32), keep_f, (0, col * cols)).reshape(-1)
    left = turn_sum(left, X_TURNS)
    left = left + move(left, SWAP_YL)

    flags = lax.dynamic_update_slice(jnp.zeros((grid, cols), F32), keep_f, (row * rows, 0))
    sums = jnp.concatenate([sums[0], flags.reshape(-1)])
    sums = row_sum(sums)
    colsum, right = sums[:width], sums[width:]
    a = (masked / colsum[None, :]).astype(BF16)
    a, left = lax.optimization_barrier((a, left))

    half = height // 2
    mine = lax.dynamic_slice(a, (c * half, 0), (half, width))
    theirs = lax.dynamic_slice(a, ((1 - c) * half, 0), (half, width))
    b = jnp.concatenate([mine, move(theirs, SWAP_CORE)], axis=1)
    notes = jnp.concatenate([left, right, keep_out.astype(F32).reshape(-1)])
    notes_o = move(notes, SWAP_CORE)

    xl, xr, pa = move(a, X_UP), move(a, X_DOWN), move(a, SWAP_YL)
    zl, zr = move(b, Z_UP), move(b, Z_DOWN)
    a, b, xl, xr, pa, zl, zr = lax.optimization_barrier((a, b, xl, xr, pa, zl, zr))
    pxl, pxr = move(pa, X_UP), move(pa, X_DOWN)
    zf, pb = move(zl, Z_UP), move(b, SWAP_YH)
    a, b, xl, xr, pa, zl, zr, pxl, pxr, zf, pb, notes_o, left, right = lax.optimization_barrier(
        (a, b, xl, xr, pa, zl, zr, pxl, pxr, zf, pb, notes_o, left, right)
    )
    xf, pxf = move(xl, X_UP), move(pxr, X_DOWN)
    pzl, pzr, pzf = move(pb, Z_UP), move(pb, Z_DOWN), move(zf, SWAP_YH)

    plan = planned(rows, cols, left, right, keep_out.astype(F32).reshape(-1), notes_o)
    a_units = [a, xl, xr, pa, pxl, pxr, xf, pxf]
    b_units = [b, zl, zr, zf, pb, pzl, pzr, pzf]
    wide = NC * cols
    mine, theirs = product(plan, a_units[:6], b_units[:5], rows, wide, tuple(range(wide)))
    theirs, = product(plan, a_units, b_units, rows, wide, tuple(range(cols, wide)), theirs)
    got = move(theirs, SWAP_CORE)
    mine, = product(plan, a_units, b_units, rows, wide, tuple(range(cols)), mine)
    inflated, total = squared(mine, got)
    total = row_sum(total[0])
    return rescaled(float(height * lax.axis_size("row")), inflated, total[None, :])


def solution(mesh):
    return jax.shard_map(
        shards,
        mesh=mesh,
        in_specs=(P("row", "col"), P("row", "col"), P("row", "col")),
        out_specs=P("row", "col"),
        check_vma=False,
    )
```

```python
import functools
import jax
import jax.numpy as jnp
from jax import lax
from jax.experimental import pallas as pl
from jax.experimental.pallas import tpu as pltpu
from jax.sharding import PartitionSpec as P

AXES = ("row", "col")
YH, NZ, YL, NX, NC = 2, 4, 2, 4, 2
F32 = jnp.float32
BF16 = jnp.bfloat16
I32 = jnp.int32
GROUP = 2


def place(yh, z, yl, x, c):
    return (yh * NZ + z) * (YL * NX * NC) + (yl * NX + x) * NC + c


def pairs(step):
    return [
        (place(yh, z, yl, x, c), place(*step(yh, z, yl, x, c)))
        for yh in range(YH)
        for z in range(NZ)
        for yl in range(YL)
        for x in range(NX)
        for c in range(NC)
    ]


X_UP = pairs(lambda yh, z, yl, x, c: (yh, z, yl, (x + 1) % NX, c))
X_DOWN = pairs(lambda yh, z, yl, x, c: (yh, z, yl, (x - 1) % NX, c))
Z_UP = pairs(lambda yh, z, yl, x, c: (yh, (z + 1) % NZ, yl, x, c))
Z_DOWN = pairs(lambda yh, z, yl, x, c: (yh, (z - 1) % NZ, yl, x, c))
SWAP_CORE = pairs(lambda yh, z, yl, x, c: (yh, z, yl, x, 1 - c))
SWAP_YL = pairs(lambda yh, z, yl, x, c: (yh, z, 1 - yl, x, c))
SWAP_YH = pairs(lambda yh, z, yl, x, c: (1 - yh, z, yl, x, c))
Z_TURNS = [pairs(lambda yh, z, yl, x, c, d=d: (yh, (z + d) % NZ, yl, x, c)) for d in range(1, NZ)]


def move(value, perm):
    return lax.ppermute(value, AXES, perm)


def turn_sum(value, turns):
    return value + sum(move(value, turn) for turn in turns)


def row_sum(value):
    value = turn_sum(value, Z_TURNS)
    return value + move(value, SWAP_YH)


def after(value, *deps):
    return lax.optimization_barrier((value, *deps))[0]


def vmem_limit(mib):
    return pltpu.CompilerParams(vmem_limit_bytes=mib * 2**20)


VMEM = pl.BlockSpec(memory_space=pltpu.VMEM)
SMEM = pl.BlockSpec(memory_space=pltpu.SMEM)
ANY = pl.BlockSpec(memory_space=pl.ANY)


def mask_kernel(keep_ref, entries_ref, masked_ref, sum_ref):
    cols, rows = keep_ref.shape
    tall, wide = entries_ref.shape[0] // rows, entries_ref.shape[1] // cols
    for j in range(cols):
        right = slice(j * wide, (j + 1) * wide)
        total = jnp.zeros((1, wide), F32)
        for i in range(rows):
            down = slice(i * tall, (i + 1) * tall)
            masked = entries_ref[down, right] * keep_ref[j, i].astype(F32)
            masked_ref[down, right] = masked
            total = total + jnp.sum(masked, axis=0, keepdims=True)
        sum_ref[:, right] = total


def mask(keep, entries):
    return pl.pallas_call(
        mask_kernel,
        out_shape=(
            jax.ShapeDtypeStruct(entries.shape, F32),
            jax.ShapeDtypeStruct((1, entries.shape[1]), F32),
        ),
        in_specs=[SMEM, VMEM],
        out_specs=(VMEM, VMEM),
        compiler_params=vmem_limit(16),
        name="mask",
    )(keep, entries)


def square_kernel(mine_ref, got_ref, out_ref, sum_ref):
    rows = out_ref.shape[0]
    step = rows // 4
    total = jnp.zeros(sum_ref.shape, F32)
    for r in range(0, rows, step):
        full = mine_ref[r:r + step, :] + got_ref[r:r + step, :]
        square = full * full
        out_ref[r:r + step, :] = square
        total = total + jnp.sum(square, axis=0, keepdims=True)
    sum_ref[...] = total


def squared(mine, got):
    return pl.pallas_call(
        square_kernel,
        out_shape=(
            jax.ShapeDtypeStruct(mine.shape, F32),
            jax.ShapeDtypeStruct((1, mine.shape[1]), F32),
        ),
        in_specs=[VMEM, VMEM],
        out_specs=(VMEM, VMEM),
        compiler_params=vmem_limit(16),
        name="square",
    )(mine, got)


def rescale_kernel(order, value_ref, total_ref, out_ref):
    factor = order / total_ref[...]
    rows = out_ref.shape[0]
    step = rows // 4
    for r in range(0, rows, step):
        out_ref[r:r + step, :] = value_ref[r:r + step, :] * factor


def rescaled(order, value, total):
    return pl.pallas_call(
        functools.partial(rescale_kernel, order),
        out_shape=jax.ShapeDtypeStruct(value.shape, F32),
        in_specs=[VMEM, VMEM],
        out_specs=VMEM,
        compiler_params=vmem_limit(16),
        name="rescale",
    )(value, total)


PLAN_LEFT, PLAN_RIGHT, PLAN_OUT, PLAN_LATE, PLAN_A, PLAN_B, PLAN_SIZE = 0, 4, 8, 24, 25, 33, 48
A_PLACES = [(0, 0), (0, NX - 1), (0, 1), (1, 0), (1, NX - 1), (1, 1), (0, 2), (1, 2)]
B_PLACES = [(0, 0), (0, NZ - 1), (0, 1), (0, 2), (1, 0), (1, NZ - 1), (1, 1), (1, 2)]
A_LATE, B_LATE = (6, 7), (5, 6, 7)


def plan_kernel(rows, cols, right_ref, out_ref, other_ref, *refs):
    units, (plan_ref, corner, sem) = refs[:-3], refs[-3:]
    row, col = lax.axis_index("row"), lax.axis_index("col")
    yh, z = row // NZ, row % NZ
    yl, x, c = col // (NX * NC), (col // NC) % NX, col % NC
    parts = YL * NX
    grid = parts * NC * cols
    n_right = grid * cols
    tall, wide = units[0].shape[0] // rows, units[0].shape[1] // cols

    copies = []
    for u, unit in enumerate(units):
        for i in range(rows):
            for k in range(cols):
                n = (u * rows + i) * cols + k
                source = unit.at[pl.ds(i * tall, corner.shape[1]), pl.ds(k * wide, corner.shape[2])]
                copies.append(pltpu.make_async_copy(source, corner.at[n], sem.at[n]))
    for copy in copies:
        copy.start()

    late = jnp.int32(0)
    left = [jnp.int32(0)] * rows
    whole = (1 << cols) - 1
    bases = []
    for u, (dy, dx) in enumerate(A_PLACES):
        base = ((yl + dy) % YL * NX + (x + dx) % NX) * cols
        bases.append(base)
        plan_ref[PLAN_A + u] = base
        if u in A_LATE:
            late = late | lax.shift_left(jnp.int32(whole), base)
            left = [m | lax.shift_left(jnp.int32(whole), base) for m in left]
    for u, (dy, dz) in enumerate(B_PLACES):
        base = ((yh + dy) % YH * NZ + (z + dz) % NZ) * cols
        plan_ref[PLAN_B + u] = base
        if u in B_LATE:
            late = late | lax.shift_left(jnp.int32(whole), base)
    plan_ref[PLAN_LATE] = late
    for j in range(NC * cols):
        m = jnp.int32(0)
        for q in range(parts):
            for i in range(cols):
                at = j % cols * grid + (q * NC + c) * cols + i
                flag = right_ref[at] if j < cols else other_ref[at]
                m = m + (flag > 0.5).astype(I32) * (1 << (q * cols + i))
        plan_ref[PLAN_RIGHT + j] = m
    for i in range(rows):
        for j in range(NC * cols):
            flag = out_ref[j * rows + i] if j < cols else other_ref[n_right + (j - cols) * rows + i]
            plan_ref[PLAN_OUT + i * NC * cols + j] = (flag > 0.5).astype(I32)

    for copy in copies:
        copy.wait()
    for i in range(rows):
        m = left[i]
        for u in range(len(units)):
            bits = jnp.int32(0)
            for k in range(cols):
                full = jnp.max(corner[(u * rows + i) * cols + k].astype(F32)) > 0
                bits = bits + full.astype(I32) * (1 << k)
            m = m | lax.shift_left(bits, bases[u])
        plan_ref[PLAN_LEFT + i] = m


def planned(rows, cols, right, keep_out, other, units):
    count = len(units) * rows * cols
    return pl.pallas_call(
        functools.partial(plan_kernel, rows, cols),
        out_shape=jax.ShapeDtypeStruct((PLAN_SIZE,), I32),
        in_specs=[SMEM] * 3 + [ANY] * len(units),
        out_specs=SMEM,
        scratch_shapes=[pltpu.VMEM((count, 16, 128), BF16), pltpu.SemaphoreType.DMA((count,))],
        compiler_params=vmem_limit(4),
        cost_estimate=pl.CostEstimate(flops=10**6, bytes_accessed=2**10, transcendentals=0),
        name="plan",
    )(right, keep_out, other, *units)


def product_kernel(n_a, n_b, shape, cols_out, begun, *refs):
    rows, cols, grid, tile = shape
    plan, refs = refs[0], refs[1:]
    if begun:
        start_ref, refs = refs[0], refs[1:]
    a_in, b_in, refs = refs[:n_a], refs[n_a:n_a + n_b], refs[n_a + n_b:]
    n_out = 1 if begun else 2
    out_refs, (a_buf, b_buf, acc, order, a_sem, b_sem) = refs[:n_out], refs[n_out:]
    wide = len(cols_out)
    no_a, no_b = rows * grid, wide * grid
    deep = a_in[0].shape[1] // tile

    when = plan[PLAN_LATE] if begun else ~plan[PLAN_LATE]
    used = {}
    for i in range(rows):
        for j in cols_out:
            pair = plan[PLAN_LEFT + i] & plan[PLAN_RIGHT + j] & when
            used[i, j] = jnp.where(plan[PLAN_OUT + i * cols + j] > 0, pair, 0)
    need_a = [functools.reduce(jnp.bitwise_or, [used[i, j] for j in cols_out]) for i in range(rows)]
    need_b = [functools.reduce(jnp.bitwise_or, [used[i, j] for i in range(rows)]) for j in cols_out]

    def tile_at(ref, i, j):
        return ref.at[pl.ds(i * tile, tile), pl.ds(j * tile, tile)]

    def each(act):
        for u in range(n_a):
            base = plan[PLAN_A + u]
            for i in range(rows):
                bits = lax.shift_right_logical(need_a[i], base)
                for k in range(deep):
                    @pl.when(bits & (1 << k) > 0)
                    def _(u=u, i=i, k=k, base=base):
                        slot = i * grid + base + k
                        act(pltpu.make_async_copy(tile_at(a_in[u], i, k), a_buf.at[slot], a_sem.at[slot]))
        for u in range(n_b):
            base = plan[PLAN_B + u]
            for n, j in enumerate(cols_out):
                bits = lax.shift_right_logical(need_b[n], base)
                for k in range(deep):
                    @pl.when(bits & (1 << k) > 0)
                    def _(u=u, n=n, j=j, k=k, base=base):
                        slot = n * grid + base + k
                        act(pltpu.make_async_copy(tile_at(b_in[u], k, j), b_buf.at[slot], b_sem.at[slot]))

    each(lambda copy: copy.start())
    a_buf[no_a] = jnp.zeros((tile, tile), BF16)
    b_buf[no_b] = jnp.zeros((tile, tile), BF16)
    count = {}
    for n, j in enumerate(cols_out):
        for i in range(rows):
            first = (n * rows + i) * (grid + GROUP)
            at = jnp.int32(first)
            for k in range(grid):
                order[at] = k
                at = at + (lax.shift_right_logical(used[i, j], k) & 1)
            for g in range(GROUP - 1):
                order[at + g] = grid
            count[i, j] = (at - first + GROUP - 1) // GROUP
    each(lambda copy: copy.wait())

    for n, j in enumerate(cols_out):
        out_ref = out_refs[n * n_out // wide]
        place = n % (wide // n_out)
        for i in range(rows):
            here = slice(i * tile, (i + 1) * tile), slice(place * tile, (place + 1) * tile)
            acc[...] = start_ref[here] if begun else jnp.zeros_like(acc)

            def step(m, _, i=i, n=n):
                part = None
                for g in range(GROUP):
                    k = order[(n * rows + i) * (grid + GROUP) + m * GROUP + g]
                    a_tile = a_buf[jnp.where(k < grid, i * grid + k, no_a)]
                    b_tile = b_buf[jnp.where(k < grid, n * grid + k, no_b)]
                    dot = jnp.dot(a_tile, b_tile, preferred_element_type=F32)
                    part = dot if part is None else part + dot
                acc[...] += part
                return 0

            lax.fori_loop(0, count[i, j], step, 0)
            out_ref[here] = acc[...]


def product(plan, a_units, b_units, rows, cols, cols_out, start=None):
    begun = start is not None
    tile = a_units[0].shape[0] // rows
    grid = YL * NX * (a_units[0].shape[1] // tile)
    half = jax.ShapeDtypeStruct((rows * tile, cols // NC * tile), F32)
    n_out = 1 if begun else NC
    return pl.pallas_call(
        functools.partial(product_kernel, len(a_units), len(b_units), (rows, cols, grid, tile), cols_out, begun),
        out_shape=(half,) * n_out,
        in_specs=[SMEM] + [VMEM] * begun + [ANY] * (len(a_units) + len(b_units)),
        out_specs=(VMEM,) * n_out,
        scratch_shapes=[
            pltpu.VMEM((rows * grid + 1, tile, tile), BF16),
            pltpu.VMEM((len(cols_out) * grid + 1, tile, tile), BF16),
            pltpu.VMEM((tile, tile), F32),
            pltpu.SMEM((rows * len(cols_out) * (grid + GROUP),), I32),
            pltpu.SemaphoreType.DMA((rows * grid,)),
            pltpu.SemaphoreType.DMA((len(cols_out) * grid,)),
        ],
        compiler_params=vmem_limit(26),
        cost_estimate=pl.CostEstimate(flops=10**6, bytes_accessed=2**10, transcendentals=0),
        name="finish" if begun else "begin",
    )(plan, *([start] if begun else []), *a_units, *b_units)


def tile_keep(flags):
    tile_rows, tile_cols = flags.shape
    row_ids = lax.axis_index("row") * tile_rows + jnp.arange(tile_rows, dtype=I32)
    col_ids = lax.axis_index("col") * tile_cols + jnp.arange(tile_cols, dtype=I32)
    diagonal = (col_ids[:, None] == row_ids[None, :]).astype(I32)
    return jnp.maximum(flags.T, diagonal)


def shards(entries, pattern, prune):
    row, col = lax.axis_index("row"), lax.axis_index("col")
    rows, cols = pattern.shape
    height, width = entries.shape
    grid = rows * lax.axis_size("row")
    c = col % NC

    keep = tile_keep(pattern)
    keep_out = tile_keep(prune)
    masked, sums = mask(keep, entries)

    flags = lax.dynamic_update_slice(jnp.zeros((cols, grid), F32), keep.astype(F32), (0, row * rows))
    sums = jnp.concatenate([sums[0], flags.reshape(-1)])
    sums = row_sum(sums)
    colsum, right = sums[:width], sums[width:]
    a = (masked / colsum[None, :]).astype(BF16)

    half = height // 2
    mine = lax.dynamic_slice(a, (c * half, 0), (half, width))
    theirs = lax.dynamic_slice(a, ((1 - c) * half, 0), (half, width))
    b = jnp.concatenate([mine, move(theirs, SWAP_CORE)], axis=1)
    kept = keep_out.astype(F32).reshape(-1)
    notes = jnp.concatenate([right, kept])
    notes_o = move(notes, SWAP_CORE)

    xl, xr, pa = move(a, X_UP), move(a, X_DOWN), move(a, SWAP_YL)
    zl, zr = move(b, Z_UP), move(b, Z_DOWN)
    pxl, pxr = move(after(pa, xl), X_UP), move(after(pa, xr), X_DOWN)
    zf, pb = move(zl, Z_UP), move(after(b, pa, zr), SWAP_YH)
    xf, pxf = move(after(xl, pxl), X_UP), move(pxr, X_DOWN)
    pzl, pzr, pzf = move(after(pb, zf), Z_UP), move(pb, Z_DOWN), move(after(zf, pb), SWAP_YH)
    notes_o, right = after(notes_o, pxl, pxr, pb), after(right, pxl, pxr, pb)

    a_units = [a, xl, xr, pa, pxl, pxr, xf, pxf]
    plan = planned(rows, cols, right, kept, notes_o, a_units[:6])
    b_units = [b, zl, zr, zf, pb, pzl, pzr, pzf]
    wide = NC * cols
    mine, theirs = product(plan, a_units[:6], b_units[:5], rows, wide, tuple(range(wide)))
    theirs, = product(plan, a_units, b_units, rows, wide, tuple(range(cols, wide)), theirs)
    got = move(theirs, SWAP_CORE)
    mine, = product(plan, a_units, b_units, rows, wide, tuple(range(cols)), mine)
    inflated, total = squared(mine, got)
    total = row_sum(total[0])
    return rescaled(float(height * lax.axis_size("row")), inflated, total[None, :])


def solution(mesh):
    return jax.shard_map(
        shards,
        mesh=mesh,
        in_specs=(P("row", "col"), P("row", "col"), P("row", "col")),
        out_specs=P("row", "col"),
        check_vma=False,
    )
```

```python
import functools
import jax
import jax.numpy as jnp
from jax import lax
from jax.experimental import pallas as pl
from jax.experimental.pallas import tpu as pltpu
from jax.sharding import PartitionSpec as P

AXES = ("row", "col")
YH, NZ, YL, NX, NC = 2, 4, 2, 4, 2
F32 = jnp.float32
BF16 = jnp.bfloat16
I32 = jnp.int32
GROUP = 4


def place(yh, z, yl, x, c):
    return (yh * NZ + z) * (YL * NX * NC) + (yl * NX + x) * NC + c


def pairs(step, cores=range(NC)):
    return [
        (place(yh, z, yl, x, c), place(*step(yh, z, yl, x, c)))
        for yh in range(YH)
        for z in range(NZ)
        for yl in range(YL)
        for x in range(NX)
        for c in cores
    ]


X_UP = pairs(lambda yh, z, yl, x, c: (yh, z, yl, (x + 1) % NX, c))
X_DOWN = pairs(lambda yh, z, yl, x, c: (yh, z, yl, (x - 1) % NX, c))
Z_UP = pairs(lambda yh, z, yl, x, c: (yh, (z + 1) % NZ, yl, x, c))
Z_DOWN = pairs(lambda yh, z, yl, x, c: (yh, (z - 1) % NZ, yl, x, c))
SWAP_CORE = pairs(lambda yh, z, yl, x, c: (yh, z, yl, x, 1 - c))
SWAP_YL = pairs(lambda yh, z, yl, x, c: (yh, z, 1 - yl, x, c))
SWAP_YH = pairs(lambda yh, z, yl, x, c: (1 - yh, z, yl, x, c))
FAR_1 = [
    pairs(lambda yh, z, yl, x, c, dy=dy: (yh, z, (yl + dy) % YL, (x + 2) % NX, c), cores=(1,))
    for dy in (0, 1)
]
Z_TURNS = [pairs(lambda yh, z, yl, x, c, d=d: (yh, (z + d) % NZ, yl, x, c)) for d in range(1, NZ)]


def move(value, perm):
    return lax.ppermute(value, AXES, perm)


def turn_sum(value, turns):
    return value + sum(move(value, turn) for turn in turns)


def row_sum(value):
    value = turn_sum(value, Z_TURNS)
    return value + move(value, SWAP_YH)


def after(value, *deps):
    return lax.optimization_barrier((value, *deps))[0]


def vmem_limit(mib):
    return pltpu.CompilerParams(vmem_limit_bytes=mib * 2**20)


VMEM = pl.BlockSpec(memory_space=pltpu.VMEM)
SMEM = pl.BlockSpec(memory_space=pltpu.SMEM)
ANY = pl.BlockSpec(memory_space=pl.ANY)


LANES = 128


def mask_kernel(pattern_in, entries_in, masked_ref, message_ref, flags_ref, pattern_ref, entries_ref, sem):
    cols, rows = pattern_ref.shape
    tall, wide = entries_ref.shape[0] // rows, entries_ref.shape[1] // cols
    small = pltpu.make_async_copy(pattern_in, pattern_ref, sem.at[rows])
    strips = [
        pltpu.make_async_copy(
            entries_in.at[pl.ds(i * tall, tall)], entries_ref.at[pl.ds(i * tall, tall)], sem.at[i]
        )
        for i in range(rows)
    ]
    for copy in [small] + strips:
        copy.start()
    row, col = lax.axis_index("row"), lax.axis_index("col")
    grid = lax.axis_size("row") * rows
    lane = lax.broadcasted_iota(I32, (1, LANES), 1)
    column_flags = jnp.zeros((1, LANES), F32)
    flags = jnp.zeros((1, LANES), F32)
    totals = [jnp.zeros((1, wide), F32) for _ in range(cols)]
    small.wait()
    for i in range(rows):
        strips[i].wait()
        down = slice(i * tall, (i + 1) * tall)
        for j in range(cols):
            right = slice(j * wide, (j + 1) * wide)
            diagonal = (row * rows + i == col * cols + j).astype(I32)
            keep = jnp.maximum(pattern_ref[j, i], diagonal).astype(F32)
            masked = entries_ref[down, right] * keep
            masked_ref[down, right] = masked
            totals[j] = totals[j] + jnp.sum(masked, axis=0, keepdims=True)
            column_flags = jnp.where(lane == j * grid + row * rows + i, keep, column_flags)
            flags = jnp.where(lane == j * rows + i, keep, flags)
    for j in range(cols):
        message_ref[:, j * wide:(j + 1) * wide] = totals[j]
    message_ref[:, cols * wide:] = column_flags
    flags_ref[...] = flags


def mask(pattern, entries):
    return pl.pallas_call(
        mask_kernel,
        out_shape=(
            jax.ShapeDtypeStruct(entries.shape, F32),
            jax.ShapeDtypeStruct((1, entries.shape[1] + LANES), F32),
            jax.ShapeDtypeStruct((1, LANES), F32),
        ),
        in_specs=[ANY] * 2,
        out_specs=(VMEM, VMEM, VMEM),
        scratch_shapes=[
            pltpu.SMEM(pattern.shape[::-1], I32),
            pltpu.VMEM(entries.shape, F32),
            pltpu.SemaphoreType.DMA((pattern.shape[0] + 1,)),
        ],
        compiler_params=vmem_limit(16),
        name="mask",
    )(pattern.T, entries)


def square_kernel(mine_ref, got_ref, out_ref, sum_ref):
    rows = out_ref.shape[0]
    step = rows // 4
    total = jnp.zeros(sum_ref.shape, F32)
    for r in range(0, rows, step):
        full = mine_ref[r:r + step, :] + got_ref[r:r + step, :]
        square = full * full
        out_ref[r:r + step, :] = square
        total = total + jnp.sum(square, axis=0, keepdims=True)
    sum_ref[...] = total


def squared(mine, got):
    return pl.pallas_call(
        square_kernel,
        out_shape=(
            jax.ShapeDtypeStruct(mine.shape, F32),
            jax.ShapeDtypeStruct((1, mine.shape[1]), F32),
        ),
        in_specs=[VMEM, VMEM],
        out_specs=(VMEM, VMEM),
        compiler_params=vmem_limit(16),
        name="square",
    )(mine, got)


def rescale_kernel(order, value_ref, total_ref, out_ref):
    factor = order / total_ref[...]
    rows = out_ref.shape[0]
    step = rows // 4
    for r in range(0, rows, step):
        out_ref[r:r + step, :] = value_ref[r:r + step, :] * factor


def rescaled(order, value, total):
    return pl.pallas_call(
        functools.partial(rescale_kernel, order),
        out_shape=jax.ShapeDtypeStruct(value.shape, F32),
        in_specs=[VMEM, VMEM],
        out_specs=VMEM,
        compiler_params=vmem_limit(16),
        name="rescale",
    )(value, total)


PLAN_LEFT, PLAN_RIGHT, PLAN_OUT, PLAN_LATE, PLAN_A, PLAN_B, PLAN_SIZE = 0, 4, 8, 24, 25, 33, 48
A_PLACES = [(0, 0), (0, NX - 1), (0, 1), (1, 0), (1, NX - 1), (1, 1), (0, 2), (1, 2)]
B_PLACES = [(0, 0), (0, NZ - 1), (0, 1), (0, 2), (1, 0), (1, NZ - 1), (1, 1), (1, 2)]
A_LATE, B_LATE = (6, 7), (5, 6, 7)


def plan_kernel(rows, cols, far_ref, right_ref, out_ref, other_ref, *refs):
    units, (plan_ref, corner, sem) = refs[:-3], refs[-3:]
    row, col = lax.axis_index("row"), lax.axis_index("col")
    yh, z = row // NZ, row % NZ
    yl, x, c = col // (NX * NC), (col // NC) % NX, col % NC
    parts = YL * NX
    grid = parts * NC * cols
    n_right = grid * cols
    n_other = n_right + rows * cols
    tall, wide = units[0].shape[0] // rows, units[0].shape[1] // cols

    copies = []
    for u, unit in enumerate(units):
        for i in range(rows):
            for k in range(cols):
                n = (u * rows + i) * cols + k
                source = unit.at[pl.ds(i * tall, corner.shape[1]), pl.ds(k * wide, corner.shape[2])]
                copies.append(pltpu.make_async_copy(source, corner.at[n], sem.at[n]))
    for copy in copies:
        copy.start()

    late = jnp.int32(0)
    left = [jnp.int32(0)] * rows
    whole = (1 << cols) - 1
    bases = []
    for u, (dy, dx) in enumerate(A_PLACES):
        base = ((yl + dy) % YL * NX + (x + dx) % NX) * cols
        bases.append(base)
        plan_ref[PLAN_A + u] = base
        if u in A_LATE:
            late = late | lax.shift_left(jnp.int32(whole), base)
            first = (A_LATE.index(u) + len(FAR_1) - len(A_LATE)) * NC * rows * cols
            for i in range(rows):
                bits = jnp.int32(0)
                for k in range(cols):
                    if first < 0:
                        bits = jnp.int32(whole)
                    else:
                        at = first + k * rows + i
                        flag = jnp.where(c == 1, far_ref[at], other_ref[n_other + rows * cols + at])
                        bits = bits + (flag > 0.5).astype(I32) * (1 << k)
                left[i] = left[i] | lax.shift_left(bits, base)
    for u, (dy, dz) in enumerate(B_PLACES):
        base = ((yh + dy) % YH * NZ + (z + dz) % NZ) * cols
        plan_ref[PLAN_B + u] = base
        if u in B_LATE:
            late = late | lax.shift_left(jnp.int32(whole), base)
    plan_ref[PLAN_LATE] = late
    for j in range(NC * cols):
        m = jnp.int32(0)
        for q in range(parts):
            for i in range(cols):
                at = j % cols * grid + (q * NC + c) * cols + i
                flag = right_ref[at] if j < cols else other_ref[at]
                m = m + (flag > 0.5).astype(I32) * (1 << (q * cols + i))
        plan_ref[PLAN_RIGHT + j] = m
    for i in range(rows):
        for j in range(NC * cols):
            flag = out_ref[j * rows + i] if j < cols else other_ref[n_right + (j - cols) * rows + i]
            plan_ref[PLAN_OUT + i * NC * cols + j] = (flag > 0.5).astype(I32)

    for copy in copies:
        copy.wait()
    for i in range(rows):
        m = left[i]
        for u in range(len(units)):
            bits = jnp.int32(0)
            for k in range(cols):
                full = jnp.max(corner[(u * rows + i) * cols + k].astype(F32)) > 0
                bits = bits + full.astype(I32) * (1 << k)
            m = m | lax.shift_left(bits, bases[u])
        plan_ref[PLAN_LEFT + i] = m


def planned(rows, cols, far, right, keep_out, other, units):
    count = len(units) * rows * cols
    return pl.pallas_call(
        functools.partial(plan_kernel, rows, cols),
        out_shape=jax.ShapeDtypeStruct((PLAN_SIZE,), I32),
        in_specs=[SMEM] * 4 + [ANY] * len(units),
        out_specs=SMEM,
        scratch_shapes=[pltpu.VMEM((count, 16, 128), BF16), pltpu.SemaphoreType.DMA((count,))],
        compiler_params=vmem_limit(4),
        cost_estimate=pl.CostEstimate(flops=10**6, bytes_accessed=2**10, transcendentals=0),
        name="plan",
    )(far, right, keep_out, other, *units)


def product_kernel(n_a, n_b, shape, cols_out, begun, *refs):
    rows, cols, grid, tile = shape
    plan, refs = refs[0], refs[1:]
    refs = refs[begun:]
    a_in, b_in, refs = refs[:n_a], refs[n_a:n_a + n_b], refs[n_a + n_b:]
    n_out = 1 if begun else 2
    out_refs, (a_buf, b_buf, order, a_sem, b_sem) = refs[:n_out], refs[n_out:]
    wide = len(cols_out)
    no_a, no_b = rows * grid, wide * grid
    deep = a_in[0].shape[1] // tile

    when = plan[PLAN_LATE] if begun else ~plan[PLAN_LATE]
    used = {}
    for i in range(rows):
        for j in cols_out:
            pair = plan[PLAN_LEFT + i] & plan[PLAN_RIGHT + j] & when
            used[i, j] = jnp.where(plan[PLAN_OUT + i * cols + j] > 0, pair, 0)
    need_a = [functools.reduce(jnp.bitwise_or, [used[i, j] for j in cols_out]) for i in range(rows)]
    need_b = [functools.reduce(jnp.bitwise_or, [used[i, j] for i in range(rows)]) for j in cols_out]

    def tile_at(ref, i, j):
        return ref.at[pl.ds(i * tile, tile), pl.ds(j * tile, tile)]

    def each(act):
        for u in range(n_a):
            base = plan[PLAN_A + u]
            bits = [lax.shift_right_logical(m, base) & ((1 << deep) - 1) for m in need_a]

            @pl.when(functools.reduce(jnp.bitwise_or, bits) > 0)
            def _(u=u, base=base, bits=bits):
                for i in range(rows):
                    for k in range(deep):
                        @pl.when(bits[i] & (1 << k) > 0)
                        def _(i=i, k=k):
                            slot = i * grid + base + k
                            act(pltpu.make_async_copy(tile_at(a_in[u], i, k), a_buf.at[slot], a_sem.at[slot]))
        for u in range(n_b):
            base = plan[PLAN_B + u]
            bits = [lax.shift_right_logical(m, base) & ((1 << deep) - 1) for m in need_b]

            @pl.when(functools.reduce(jnp.bitwise_or, bits) > 0)
            def _(u=u, base=base, bits=bits):
                for n, j in enumerate(cols_out):
                    for k in range(deep):
                        @pl.when(bits[n] & (1 << k) > 0)
                        def _(n=n, j=j, k=k):
                            slot = n * grid + base + k
                            act(pltpu.make_async_copy(tile_at(b_in[u], k, j), b_buf.at[slot], b_sem.at[slot]))

    each(lambda copy: copy.start())
    a_buf[no_a] = jnp.zeros((tile, tile), BF16)
    b_buf[no_b] = jnp.zeros((tile, tile), BF16)
    count = {}
    for n, j in enumerate(cols_out):
        for i in range(rows):
            first = (n * rows + i) * (grid + GROUP)
            at = jnp.int32(first)
            for k in range(grid):
                order[at] = k
                at = at + (lax.shift_right_logical(used[i, j], k) & 1)
            for g in range(GROUP - 1):
                order[at + g] = grid
            count[i, j] = (at - first + GROUP - 1) // GROUP
    each(lambda copy: copy.wait())

    for n, j in enumerate(cols_out):
        out_ref = out_refs[n * n_out // wide]
        place = n % (wide // n_out)
        for i in range(rows):
            here = slice(i * tile, (i + 1) * tile), slice(place * tile, (place + 1) * tile)
            if not begun:
                out_ref[here] = jnp.zeros((tile, tile), F32)

            def step(m, _, i=i, n=n, here=here, out_ref=out_ref):
                part = None
                for g in range(GROUP):
                    k = order[(n * rows + i) * (grid + GROUP) + m * GROUP + g]
                    a_tile = a_buf[jnp.where(k < grid, i * grid + k, no_a)]
                    b_tile = b_buf[jnp.where(k < grid, n * grid + k, no_b)]
                    dot = jnp.dot(a_tile, b_tile, preferred_element_type=F32)
                    part = dot if part is None else part + dot
                out_ref[here] += part
                return 0

            lax.fori_loop(0, count[i, j], step, 0)


def product(plan, a_units, b_units, rows, cols, cols_out, start=None):
    begun = start is not None
    tile = a_units[0].shape[0] // rows
    grid = YL * NX * (a_units[0].shape[1] // tile)
    half = jax.ShapeDtypeStruct((rows * tile, cols // NC * tile), F32)
    n_out = 1 if begun else NC
    return pl.pallas_call(
        functools.partial(product_kernel, len(a_units), len(b_units), (rows, cols, grid, tile), cols_out, begun),
        out_shape=(half,) * n_out,
        in_specs=[SMEM] + [VMEM] * begun + [ANY] * (len(a_units) + len(b_units)),
        out_specs=(VMEM,) * n_out,
        scratch_shapes=[
            pltpu.VMEM((rows * grid + 1, tile, tile), BF16),
            pltpu.VMEM((len(cols_out) * grid + 1, tile, tile), BF16),
            pltpu.SMEM((rows * len(cols_out) * (grid + GROUP),), I32),
            pltpu.SemaphoreType.DMA((rows * grid,)),
            pltpu.SemaphoreType.DMA((len(cols_out) * grid,)),
        ],
        compiler_params=vmem_limit(26),
        cost_estimate=pl.CostEstimate(flops=10**6, bytes_accessed=2**10, transcendentals=0),
        input_output_aliases={1: 0} if begun else {},
        name="finish" if begun else "begin",
    )(plan, *([start] if begun else []), *a_units, *b_units)


def shards(entries, pattern, prune):
    col = lax.axis_index("col")
    rows, cols = pattern.shape
    height, width = entries.shape
    grid = rows * lax.axis_size("row")
    c = col % NC

    masked, message, flags = mask(pattern, entries)
    flags = flags[0, :rows * cols]
    row_ids = lax.axis_index("row") * rows + jnp.arange(rows, dtype=I32)
    col_ids = col * cols + jnp.arange(cols, dtype=I32)
    diagonal = (col_ids[:, None] == row_ids[None, :]).astype(I32)
    kept = jnp.maximum(prune.T, diagonal).astype(F32).reshape(-1)

    message = row_sum(message)
    colsum, right = message[:, :width], message[0, width:width + grid * cols]
    a = (masked / colsum).astype(BF16)

    half = height // 2
    mine = lax.dynamic_slice(a, (c * half, 0), (half, width))
    theirs = lax.dynamic_slice(a, ((1 - c) * half, 0), (half, width))
    b = jnp.concatenate([mine, move(theirs, SWAP_CORE)], axis=1)

    flags = after(jnp.concatenate([flags, move(flags, SWAP_CORE)]), b)
    far = jnp.concatenate([move(flags, far) for far in FAR_1])
    a, b, far = lax.optimization_barrier((a, b, far))
    notes_o = move(jnp.concatenate([right, kept, far]), SWAP_CORE)

    xl, xr, pa = move(a, X_UP), move(a, X_DOWN), move(a, SWAP_YL)
    zl, zr = move(b, Z_UP), move(b, Z_DOWN)
    pxl, pxr = move(after(pa, xl), X_UP), move(after(pa, xr), X_DOWN)
    zf, pb = move(zl, Z_UP), move(after(b, pa, zr), SWAP_YH)
    xf, pxf = move(after(xl, pxl), X_UP), move(pxr, X_DOWN)
    pzl, pzr, pzf = move(after(pb, zf), Z_UP), move(pb, Z_DOWN), move(after(zf, pb), SWAP_YH)
    notes_o, far, right = after(notes_o, pxl, pxr, pb), after(far, pxl, pxr, pb), after(right, pxl, pxr, pb)

    a_units = [a, xl, xr, pa, pxl, pxr, xf, pxf]
    plan = planned(rows, cols, far, right, kept, notes_o, a_units[:6])
    b_units = [b, zl, zr, zf, pb, pzl, pzr, pzf]
    wide = NC * cols
    mine, theirs = product(plan, a_units[:6], b_units[:5], rows, wide, tuple(range(wide)))
    theirs, = product(plan, a_units, b_units, rows, wide, tuple(range(cols, wide)), theirs)
    got = move(theirs, SWAP_CORE)
    mine, = product(plan, a_units, b_units, rows, wide, tuple(range(cols)), mine)
    inflated, total = squared(mine, got)
    total = row_sum(total)
    return rescaled(float(height * lax.axis_size("row")), inflated, total)


def solution(mesh):
    return jax.shard_map(
        shards,
        mesh=mesh,
        in_specs=(P("row", "col"), P("row", "col"), P("row", "col")),
        out_specs=P("row", "col"),
        check_vma=False,
    )
```

```python
import functools
import jax
import jax.numpy as jnp
from jax import lax
from jax.experimental import pallas as pl
from jax.experimental.pallas import tpu as pltpu
from jax.sharding import PartitionSpec as P

AXES = ("row", "col")
YH, NZ, YL, NX, NC = 2, 4, 2, 4, 2
F32 = jnp.float32
BF16 = jnp.bfloat16
I32 = jnp.int32
GROUP = 4


def place(yh, z, yl, x, c):
    return (yh * NZ + z) * (YL * NX * NC) + (yl * NX + x) * NC + c


def pairs(step, cores=range(NC)):
    return [
        (place(yh, z, yl, x, c), place(*step(yh, z, yl, x, c)))
        for yh in range(YH)
        for z in range(NZ)
        for yl in range(YL)
        for x in range(NX)
        for c in cores
    ]


X_UP = pairs(lambda yh, z, yl, x, c: (yh, z, yl, (x + 1) % NX, c))
X_DOWN = pairs(lambda yh, z, yl, x, c: (yh, z, yl, (x - 1) % NX, c))
Z_UP = pairs(lambda yh, z, yl, x, c: (yh, (z + 1) % NZ, yl, x, c))
Z_DOWN = pairs(lambda yh, z, yl, x, c: (yh, (z - 1) % NZ, yl, x, c))
SWAP_CORE = pairs(lambda yh, z, yl, x, c: (yh, z, yl, x, 1 - c))
SWAP_YL = pairs(lambda yh, z, yl, x, c: (yh, z, 1 - yl, x, c))
SWAP_YH = pairs(lambda yh, z, yl, x, c: (1 - yh, z, yl, x, c))
FAR_1 = [
    pairs(lambda yh, z, yl, x, c, dy=dy: (yh, z, (yl + dy) % YL, (x + 2) % NX, c), cores=(1,))
    for dy in (0, 1)
]
Z_TURNS = [pairs(lambda yh, z, yl, x, c, d=d: (yh, (z + d) % NZ, yl, x, c)) for d in range(1, NZ)]


def move(value, perm):
    return lax.ppermute(value, AXES, perm)


def turn_sum(value, turns):
    return value + sum(move(value, turn) for turn in turns)


def row_sum(value, *beside):
    value = turn_sum(value, Z_TURNS)
    if beside:
        value = after(value, *beside)
    return value + move(value, SWAP_YH)


def after(value, *deps):
    return lax.optimization_barrier((value, *deps))[0]


def vmem_limit(mib):
    return pltpu.CompilerParams(vmem_limit_bytes=mib * 2**20)


VMEM = pl.BlockSpec(memory_space=pltpu.VMEM)
SMEM = pl.BlockSpec(memory_space=pltpu.SMEM)
ANY = pl.BlockSpec(memory_space=pl.ANY)


LANES = 128


def mask_kernel(pattern_in, entries_in, masked_ref, message_ref, flags_ref, pattern_ref, entries_ref, sem):
    cols, rows = pattern_ref.shape
    tall, wide = entries_ref.shape[0] // rows, entries_ref.shape[1] // cols
    small = pltpu.make_async_copy(pattern_in, pattern_ref, sem.at[rows])
    strips = [
        pltpu.make_async_copy(
            entries_in.at[pl.ds(i * tall, tall)], entries_ref.at[pl.ds(i * tall, tall)], sem.at[i]
        )
        for i in range(rows)
    ]
    for copy in [small] + strips:
        copy.start()
    row, col = lax.axis_index("row"), lax.axis_index("col")
    grid = lax.axis_size("row") * rows
    lane = lax.broadcasted_iota(I32, (1, LANES), 1)
    column_flags = jnp.zeros((1, LANES), F32)
    flags = jnp.zeros((1, LANES), F32)
    totals = [jnp.zeros((1, wide), F32) for _ in range(cols)]
    small.wait()
    for i in range(rows):
        strips[i].wait()
        down = slice(i * tall, (i + 1) * tall)
        for j in range(cols):
            right = slice(j * wide, (j + 1) * wide)
            diagonal = (row * rows + i == col * cols + j).astype(I32)
            keep = jnp.maximum(pattern_ref[j, i], diagonal).astype(F32)
            masked = entries_ref[down, right] * keep
            masked_ref[down, right] = masked
            totals[j] = totals[j] + jnp.sum(masked, axis=0, keepdims=True)
            column_flags = jnp.where(lane == j * grid + row * rows + i, keep, column_flags)
            flags = jnp.where(lane == j * rows + i, keep, flags)
    for j in range(cols):
        message_ref[:, j * wide:(j + 1) * wide] = totals[j]
    message_ref[:, cols * wide:] = column_flags
    flags_ref[...] = flags


def mask(pattern, entries):
    return pl.pallas_call(
        mask_kernel,
        out_shape=(
            jax.ShapeDtypeStruct(entries.shape, F32),
            jax.ShapeDtypeStruct((1, entries.shape[1] + LANES), F32),
            jax.ShapeDtypeStruct((1, LANES), F32),
        ),
        in_specs=[ANY] * 2,
        out_specs=(VMEM, VMEM, VMEM),
        scratch_shapes=[
            pltpu.SMEM(pattern.shape[::-1], I32),
            pltpu.VMEM(entries.shape, F32),
            pltpu.SemaphoreType.DMA((pattern.shape[0] + 1,)),
        ],
        compiler_params=vmem_limit(16),
        name="mask",
    )(pattern.T, entries)


def square_kernel(mine_ref, got_ref, out_ref, sum_ref):
    rows = out_ref.shape[0]
    step = rows // 4
    total = jnp.zeros(sum_ref.shape, F32)
    for r in range(0, rows, step):
        full = mine_ref[r:r + step, :] + got_ref[r:r + step, :]
        square = full * full
        out_ref[r:r + step, :] = square
        total = total + jnp.sum(square, axis=0, keepdims=True)
    sum_ref[...] = total


def squared(mine, got):
    return pl.pallas_call(
        square_kernel,
        out_shape=(
            jax.ShapeDtypeStruct(mine.shape, F32),
            jax.ShapeDtypeStruct((1, mine.shape[1]), F32),
        ),
        in_specs=[VMEM, VMEM],
        out_specs=(VMEM, VMEM),
        compiler_params=vmem_limit(16),
        name="square",
    )(mine, got)


def rescale_kernel(order, value_ref, total_ref, out_ref):
    factor = order / total_ref[...]
    rows = out_ref.shape[0]
    step = rows // 4
    for r in range(0, rows, step):
        out_ref[r:r + step, :] = value_ref[r:r + step, :] * factor


def rescaled(order, value, total):
    return pl.pallas_call(
        functools.partial(rescale_kernel, order),
        out_shape=jax.ShapeDtypeStruct(value.shape, F32),
        in_specs=[VMEM, VMEM],
        out_specs=VMEM,
        compiler_params=vmem_limit(16),
        name="rescale",
    )(value, total)


PLAN_LEFT, PLAN_RIGHT, PLAN_OUT, PLAN_LATE, PLAN_A, PLAN_B, PLAN_SIZE = 0, 4, 8, 24, 25, 33, 48
A_PLACES = [(0, 0), (0, NX - 1), (0, 1), (1, 0), (1, NX - 1), (1, 1), (0, 2), (1, 2)]
B_PLACES = [(0, 0), (0, NZ - 1), (0, 1), (0, 2), (1, 0), (1, NZ - 1), (1, 1), (1, 2)]
A_LATE, B_LATE = (6, 7), (5, 6, 7)


def plan_kernel(rows, cols, far_ref, right_ref, out_ref, other_ref, *refs):
    units, (plan_ref, corner, sem) = refs[:-3], refs[-3:]
    row, col = lax.axis_index("row"), lax.axis_index("col")
    yh, z = row // NZ, row % NZ
    yl, x, c = col // (NX * NC), (col // NC) % NX, col % NC
    parts = YL * NX
    grid = parts * NC * cols
    n_right = grid * cols
    n_other = n_right + rows * cols
    tall, wide = units[0].shape[0] // rows, units[0].shape[1] // cols

    copies = []
    for u, unit in enumerate(units):
        for i in range(rows):
            for k in range(cols):
                n = (u * rows + i) * cols + k
                source = unit.at[pl.ds(i * tall, corner.shape[1]), pl.ds(k * wide, corner.shape[2])]
                copies.append(pltpu.make_async_copy(source, corner.at[n], sem.at[n]))
    for copy in copies:
        copy.start()

    late = jnp.int32(0)
    left = [jnp.int32(0)] * rows
    whole = (1 << cols) - 1
    bases = []
    for u, (dy, dx) in enumerate(A_PLACES):
        base = ((yl + dy) % YL * NX + (x + dx) % NX) * cols
        bases.append(base)
        plan_ref[PLAN_A + u] = base
        if u in A_LATE:
            late = late | lax.shift_left(jnp.int32(whole), base)
            first = (A_LATE.index(u) + len(FAR_1) - len(A_LATE)) * NC * rows * cols
            for i in range(rows):
                bits = jnp.int32(0)
                for k in range(cols):
                    if first < 0:
                        bits = jnp.int32(whole)
                    else:
                        at = first + k * rows + i
                        flag = jnp.where(c == 1, far_ref[at], other_ref[n_other + rows * cols + at])
                        bits = bits + (flag > 0.5).astype(I32) * (1 << k)
                left[i] = left[i] | lax.shift_left(bits, base)
    for u, (dy, dz) in enumerate(B_PLACES):
        base = ((yh + dy) % YH * NZ + (z + dz) % NZ) * cols
        plan_ref[PLAN_B + u] = base
        if u in B_LATE:
            late = late | lax.shift_left(jnp.int32(whole), base)
    plan_ref[PLAN_LATE] = late
    for j in range(NC * cols):
        m = jnp.int32(0)
        for q in range(parts):
            for i in range(cols):
                at = j % cols * grid + (q * NC + c) * cols + i
                flag = right_ref[at] if j < cols else other_ref[at]
                m = m + (flag > 0.5).astype(I32) * (1 << (q * cols + i))
        plan_ref[PLAN_RIGHT + j] = m
    for i in range(rows):
        for j in range(NC * cols):
            flag = out_ref[j * rows + i] if j < cols else other_ref[n_right + (j - cols) * rows + i]
            plan_ref[PLAN_OUT + i * NC * cols + j] = (flag > 0.5).astype(I32)

    for copy in copies:
        copy.wait()
    for i in range(rows):
        m = left[i]
        for u in range(len(units)):
            bits = jnp.int32(0)
            for k in range(cols):
                full = jnp.max(corner[(u * rows + i) * cols + k].astype(F32)) > 0
                bits = bits + full.astype(I32) * (1 << k)
            m = m | lax.shift_left(bits, bases[u])
        plan_ref[PLAN_LEFT + i] = m


def planned(rows, cols, far, right, keep_out, other, units):
    count = len(units) * rows * cols
    return pl.pallas_call(
        functools.partial(plan_kernel, rows, cols),
        out_shape=jax.ShapeDtypeStruct((PLAN_SIZE,), I32),
        in_specs=[SMEM] * 4 + [ANY] * len(units),
        out_specs=SMEM,
        scratch_shapes=[pltpu.VMEM((count, 16, 128), BF16), pltpu.SemaphoreType.DMA((count,))],
        compiler_params=vmem_limit(4),
        cost_estimate=pl.CostEstimate(flops=10**6, bytes_accessed=2**10, transcendentals=0),
        name="plan",
    )(far, right, keep_out, other, *units)


def product_kernel(n_a, n_b, shape, cols_out, begun, *refs):
    rows, cols, grid, tile = shape
    plan, refs = refs[0], refs[1:]
    refs = refs[begun:]
    a_in, b_in, refs = refs[:n_a], refs[n_a:n_a + n_b], refs[n_a + n_b:]
    n_out = 1 if begun else 2
    out_refs, (a_buf, b_buf, order, a_sem, b_sem) = refs[:n_out], refs[n_out:]
    wide = len(cols_out)
    no_a, no_b = rows * grid, wide * grid
    deep = a_in[0].shape[1] // tile

    when = plan[PLAN_LATE] if begun else ~plan[PLAN_LATE]
    used = {}
    for i in range(rows):
        for j in cols_out:
            pair = plan[PLAN_LEFT + i] & plan[PLAN_RIGHT + j] & when
            used[i, j] = jnp.where(plan[PLAN_OUT + i * cols + j] > 0, pair, 0)
    need_a = [functools.reduce(jnp.bitwise_or, [used[i, j] for j in cols_out]) for i in range(rows)]
    need_b = [functools.reduce(jnp.bitwise_or, [used[i, j] for i in range(rows)]) for j in cols_out]

    def tile_at(ref, i, j):
        return ref.at[pl.ds(i * tile, tile), pl.ds(j * tile, tile)]

    def each(act):
        for u in range(n_a):
            base = plan[PLAN_A + u]
            bits = [lax.shift_right_logical(m, base) & ((1 << deep) - 1) for m in need_a]

            @pl.when(functools.reduce(jnp.bitwise_or, bits) > 0)
            def _(u=u, base=base, bits=bits):
                for i in range(rows):
                    for k in range(deep):
                        @pl.when(bits[i] & (1 << k) > 0)
                        def _(i=i, k=k):
                            slot = i * grid + base + k
                            act(pltpu.make_async_copy(tile_at(a_in[u], i, k), a_buf.at[slot], a_sem.at[slot]))
        for u in range(n_b):
            base = plan[PLAN_B + u]
            bits = [lax.shift_right_logical(m, base) & ((1 << deep) - 1) for m in need_b]

            @pl.when(functools.reduce(jnp.bitwise_or, bits) > 0)
            def _(u=u, base=base, bits=bits):
                for n, j in enumerate(cols_out):
                    for k in range(deep):
                        @pl.when(bits[n] & (1 << k) > 0)
                        def _(n=n, j=j, k=k):
                            slot = n * grid + base + k
                            act(pltpu.make_async_copy(tile_at(b_in[u], k, j), b_buf.at[slot], b_sem.at[slot]))

    each(lambda copy: copy.start())
    a_buf[no_a] = jnp.zeros((tile, tile), BF16)
    b_buf[no_b] = jnp.zeros((tile, tile), BF16)
    count = {}
    for n, j in enumerate(cols_out):
        for i in range(rows):
            first = (n * rows + i) * (grid + GROUP)
            at = jnp.int32(first)
            for k in range(grid):
                order[at] = k
                at = at + (lax.shift_right_logical(used[i, j], k) & 1)
            for g in range(GROUP - 1):
                order[at + g] = grid
            count[i, j] = (at - first + GROUP - 1) // GROUP
    each(lambda copy: copy.wait())

    for n, j in enumerate(cols_out):
        out_ref = out_refs[n * n_out // wide]
        place = n % (wide // n_out)
        for i in range(rows):
            here = slice(i * tile, (i + 1) * tile), slice(place * tile, (place + 1) * tile)
            if not begun:
                out_ref[here] = jnp.zeros((tile, tile), F32)

            def step(m, _, i=i, n=n, here=here, out_ref=out_ref):
                part = None
                for g in range(GROUP):
                    k = order[(n * rows + i) * (grid + GROUP) + m * GROUP + g]
                    a_tile = a_buf[jnp.where(k < grid, i * grid + k, no_a)]
                    b_tile = b_buf[jnp.where(k < grid, n * grid + k, no_b)]
                    dot = jnp.dot(a_tile, b_tile, preferred_element_type=F32)
                    part = dot if part is None else part + dot
                out_ref[here] += part
                return 0

            lax.fori_loop(0, count[i, j], step, 0)


def product(plan, a_units, b_units, rows, cols, cols_out, start=None):
    begun = start is not None
    tile = a_units[0].shape[0] // rows
    grid = YL * NX * (a_units[0].shape[1] // tile)
    half = jax.ShapeDtypeStruct((rows * tile, cols // NC * tile), F32)
    n_out = 1 if begun else NC
    return pl.pallas_call(
        functools.partial(product_kernel, len(a_units), len(b_units), (rows, cols, grid, tile), cols_out, begun),
        out_shape=(half,) * n_out,
        in_specs=[SMEM] + [VMEM] * begun + [ANY] * (len(a_units) + len(b_units)),
        out_specs=(VMEM,) * n_out,
        scratch_shapes=[
            pltpu.VMEM((rows * grid + 1, tile, tile), BF16),
            pltpu.VMEM((len(cols_out) * grid + 1, tile, tile), BF16),
            pltpu.SMEM((rows * len(cols_out) * (grid + GROUP),), I32),
            pltpu.SemaphoreType.DMA((rows * grid,)),
            pltpu.SemaphoreType.DMA((len(cols_out) * grid,)),
        ],
        compiler_params=vmem_limit(26),
        cost_estimate=pl.CostEstimate(flops=10**6, bytes_accessed=2**10, transcendentals=0),
        input_output_aliases={1: 0} if begun else {},
        name="finish" if begun else "begin",
    )(plan, *([start] if begun else []), *a_units, *b_units)


def shards(entries, pattern, prune):
    col = lax.axis_index("col")
    rows, cols = pattern.shape
    height, width = entries.shape
    grid = rows * lax.axis_size("row")
    c = col % NC

    masked, message, flags = mask(pattern, entries)
    flags = flags[0, :rows * cols]
    row_ids = lax.axis_index("row") * rows + jnp.arange(rows, dtype=I32)
    col_ids = col * cols + jnp.arange(cols, dtype=I32)
    diagonal = (col_ids[:, None] == row_ids[None, :]).astype(I32)
    kept = jnp.maximum(prune.T, diagonal).astype(F32).reshape(-1)

    flags = jnp.concatenate([flags, move(flags, SWAP_CORE)])
    message = row_sum(message, flags)
    colsum, right = message[:, :width], message[0, width:width + grid * cols]
    a = (masked / colsum).astype(BF16)

    half = height // 2
    mine = lax.dynamic_slice(a, (c * half, 0), (half, width))
    theirs = lax.dynamic_slice(a, ((1 - c) * half, 0), (half, width))
    b = jnp.concatenate([mine, move(theirs, SWAP_CORE)], axis=1)

    flags = after(flags, a)
    far = jnp.concatenate([move(flags, far) for far in FAR_1])
    a, far = lax.optimization_barrier((a, far))
    notes_o = move(jnp.concatenate([right, kept, far]), SWAP_CORE)

    xl, xr, pa = move(a, X_UP), move(a, X_DOWN), move(a, SWAP_YL)
    zl, zr = move(after(b, far), Z_UP), move(b, Z_DOWN)
    pxl, pxr = move(after(pa, xl), X_UP), move(after(pa, xr), X_DOWN)
    zf, pb = move(after(zl, zr), Z_UP), move(after(b, pa), SWAP_YH)
    xf, pxf = move(after(xl, pxl), X_UP), move(pxr, X_DOWN)
    pzl, pzr, pzf = move(after(pb, zf), Z_UP), move(pb, Z_DOWN), move(after(zf, pb), SWAP_YH)
    notes_o, far, right = after(notes_o, pxl, pxr, pb), after(far, pxl, pxr, pb), after(right, pxl, pxr, pb)

    a_units = [a, xl, xr, pa, pxl, pxr, xf, pxf]
    plan = planned(rows, cols, far, right, kept, notes_o, a_units[:6])
    b_units = [b, zl, zr, zf, pb, pzl, pzr, pzf]
    wide = NC * cols
    mine, theirs = product(plan, a_units[:6], b_units[:5], rows, wide, tuple(range(wide)))
    theirs, = product(plan, a_units, b_units, rows, wide, tuple(range(cols, wide)), theirs)
    got = move(theirs, SWAP_CORE)
    mine, = product(plan, a_units, b_units, rows, wide, tuple(range(cols)), mine)
    inflated, total = squared(mine, got)
    total = row_sum(total)
    return rescaled(float(height * lax.axis_size("row")), inflated, total)


def solution(mesh):
    return jax.shard_map(
        shards,
        mesh=mesh,
        in_specs=(P("row", "col"), P("row", "col"), P("row", "col")),
        out_specs=P("row", "col"),
        check_vma=False,
    )
```

```python
import functools
import jax
import jax.numpy as jnp
from jax import lax
from jax.experimental import pallas as pl
from jax.experimental.pallas import tpu as pltpu
from jax.sharding import PartitionSpec as P

AXES = ("row", "col")
YH, NZ, YL, NX, NC = 2, 4, 2, 4, 2
F32 = jnp.float32
BF16 = jnp.bfloat16
I32 = jnp.int32
GROUP = 4


def place(yh, z, yl, x, c):
    return (yh * NZ + z) * (YL * NX * NC) + (yl * NX + x) * NC + c


def pairs(step, cores=range(NC)):
    return [
        (place(yh, z, yl, x, c), place(*step(yh, z, yl, x, c)))
        for yh in range(YH)
        for z in range(NZ)
        for yl in range(YL)
        for x in range(NX)
        for c in cores
    ]


X_UP = pairs(lambda yh, z, yl, x, c: (yh, z, yl, (x + 1) % NX, c))
X_DOWN = pairs(lambda yh, z, yl, x, c: (yh, z, yl, (x - 1) % NX, c))
Z_UP = pairs(lambda yh, z, yl, x, c: (yh, (z + 1) % NZ, yl, x, c))
Z_DOWN = pairs(lambda yh, z, yl, x, c: (yh, (z - 1) % NZ, yl, x, c))
SWAP_CORE = pairs(lambda yh, z, yl, x, c: (yh, z, yl, x, 1 - c))
SWAP_YL = pairs(lambda yh, z, yl, x, c: (yh, z, 1 - yl, x, c))
SWAP_YH = pairs(lambda yh, z, yl, x, c: (1 - yh, z, yl, x, c))
FAR_1 = [
    pairs(lambda yh, z, yl, x, c, dy=dy: (yh, z, (yl + dy) % YL, (x + 2) % NX, c), cores=(1,))
    for dy in (0, 1)
]
Z_TURNS = [pairs(lambda yh, z, yl, x, c, d=d: (yh, (z + d) % NZ, yl, x, c)) for d in range(1, NZ)]


def move(value, perm):
    return lax.ppermute(value, AXES, perm)


def turn_sum(value, turns):
    return value + sum(move(value, turn) for turn in turns)


def row_sum(value, *beside):
    value = turn_sum(value, Z_TURNS)
    if beside:
        value = after(value, *beside)
    return value + move(value, SWAP_YH)


def after(value, *deps):
    return lax.optimization_barrier((value, *deps))[0]


def vmem_limit(mib):
    return pltpu.CompilerParams(vmem_limit_bytes=mib * 2**20)


VMEM = pl.BlockSpec(memory_space=pltpu.VMEM)
SMEM = pl.BlockSpec(memory_space=pltpu.SMEM)
ANY = pl.BlockSpec(memory_space=pl.ANY)


LANES = 128


def mask_kernel(pattern_in, entries_in, masked_ref, message_ref, flags_ref, pattern_ref, entries_ref, sem):
    cols, rows = pattern_ref.shape
    tall, wide = entries_ref.shape[0] // rows, entries_ref.shape[1] // cols
    small = pltpu.make_async_copy(pattern_in, pattern_ref, sem.at[rows])
    strips = [
        pltpu.make_async_copy(
            entries_in.at[pl.ds(i * tall, tall)], entries_ref.at[pl.ds(i * tall, tall)], sem.at[i]
        )
        for i in range(rows)
    ]
    for copy in [small] + strips:
        copy.start()
    row, col = lax.axis_index("row"), lax.axis_index("col")
    grid = lax.axis_size("row") * rows
    lane = lax.broadcasted_iota(I32, (1, LANES), 1)
    column_flags = jnp.zeros((1, LANES), F32)
    flags = jnp.zeros((1, LANES), F32)
    totals = [jnp.zeros((1, wide), F32) for _ in range(cols)]
    small.wait()
    for i in range(rows):
        strips[i].wait()
        down = slice(i * tall, (i + 1) * tall)
        for j in range(cols):
            right = slice(j * wide, (j + 1) * wide)
            diagonal = (row * rows + i == col * cols + j).astype(I32)
            keep = jnp.maximum(pattern_ref[j, i], diagonal).astype(F32)
            masked = entries_ref[down, right] * keep
            masked_ref[down, right] = masked
            totals[j] = totals[j] + jnp.sum(masked, axis=0, keepdims=True)
            column_flags = jnp.where(lane == j * grid + row * rows + i, keep, column_flags)
            flags = jnp.where(lane == j * rows + i, keep, flags)
    for j in range(cols):
        message_ref[:, j * wide:(j + 1) * wide] = totals[j]
    message_ref[:, cols * wide:] = column_flags
    flags_ref[...] = flags


def mask(pattern, entries):
    return pl.pallas_call(
        mask_kernel,
        out_shape=(
            jax.ShapeDtypeStruct(entries.shape, F32),
            jax.ShapeDtypeStruct((1, entries.shape[1] + LANES), F32),
            jax.ShapeDtypeStruct((1, LANES), F32),
        ),
        in_specs=[ANY] * 2,
        out_specs=(VMEM, VMEM, VMEM),
        scratch_shapes=[
            pltpu.SMEM(pattern.shape[::-1], I32),
            pltpu.VMEM(entries.shape, F32),
            pltpu.SemaphoreType.DMA((pattern.shape[0] + 1,)),
        ],
        compiler_params=vmem_limit(16),
        name="mask",
    )(pattern.T, entries)


def square_kernel(mine_ref, got_ref, out_ref, sum_ref):
    rows = out_ref.shape[0]
    step = rows // 4
    total = jnp.zeros(sum_ref.shape, F32)
    for r in range(0, rows, step):
        full = mine_ref[r:r + step, :] + got_ref[r:r + step, :]
        square = full * full
        out_ref[r:r + step, :] = square
        total = total + jnp.sum(square, axis=0, keepdims=True)
    sum_ref[...] = total


def squared(mine, got):
    return pl.pallas_call(
        square_kernel,
        out_shape=(
            jax.ShapeDtypeStruct(mine.shape, F32),
            jax.ShapeDtypeStruct((1, mine.shape[1]), F32),
        ),
        in_specs=[VMEM, VMEM],
        out_specs=(VMEM, VMEM),
        compiler_params=vmem_limit(16),
        name="square",
    )(mine, got)


def rescale_kernel(order, value_ref, total_ref, out_ref):
    factor = order / total_ref[...]
    rows = out_ref.shape[0]
    step = rows // 4
    for r in range(0, rows, step):
        out_ref[r:r + step, :] = value_ref[r:r + step, :] * factor


def rescaled(order, value, total):
    return pl.pallas_call(
        functools.partial(rescale_kernel, order),
        out_shape=jax.ShapeDtypeStruct(value.shape, F32),
        in_specs=[VMEM, VMEM],
        out_specs=VMEM,
        compiler_params=vmem_limit(16),
        name="rescale",
    )(value, total)


PLAN_LEFT, PLAN_RIGHT, PLAN_OUT, PLAN_LATE, PLAN_A, PLAN_B, PLAN_SIZE = 0, 4, 8, 24, 25, 33, 48
A_PLACES = [(0, 0), (0, NX - 1), (0, 1), (1, 0), (1, NX - 1), (1, 1), (0, 2), (1, 2)]
B_PLACES = [(0, 0), (0, NZ - 1), (0, 1), (0, 2), (1, 0), (1, NZ - 1), (1, 1), (1, 2)]
A_LATE, B_LATE = (6, 7), (5, 6, 7)


def plan_kernel(rows, cols, far_ref, right_ref, out_ref, other_ref, *refs):
    units, (plan_ref, corner, sem) = refs[:-3], refs[-3:]
    row, col = lax.axis_index("row"), lax.axis_index("col")
    yh, z = row // NZ, row % NZ
    yl, x, c = col // (NX * NC), (col // NC) % NX, col % NC
    parts = YL * NX
    grid = parts * NC * cols
    n_right = grid * cols
    n_other = n_right + rows * cols
    tall, wide = units[0].shape[0] // rows, units[0].shape[1] // cols

    copies = []
    for u, unit in enumerate(units):
        for i in range(rows):
            for k in range(cols):
                n = (u * rows + i) * cols + k
                source = unit.at[pl.ds(i * tall, corner.shape[1]), pl.ds(k * wide, corner.shape[2])]
                copies.append(pltpu.make_async_copy(source, corner.at[n], sem.at[n]))
    for copy in copies:
        copy.start()

    late = jnp.int32(0)
    left = [jnp.int32(0)] * rows
    whole = (1 << cols) - 1
    bases = []
    for u, (dy, dx) in enumerate(A_PLACES):
        base = ((yl + dy) % YL * NX + (x + dx) % NX) * cols
        bases.append(base)
        plan_ref[PLAN_A + u] = base
        if u in A_LATE:
            late = late | lax.shift_left(jnp.int32(whole), base)
            first = (A_LATE.index(u) + len(FAR_1) - len(A_LATE)) * NC * rows * cols
            for i in range(rows):
                bits = jnp.int32(0)
                for k in range(cols):
                    if first < 0:
                        bits = jnp.int32(whole)
                    else:
                        at = first + k * rows + i
                        flag = jnp.where(c == 1, far_ref[at], other_ref[n_other + rows * cols + at])
                        bits = bits + (flag > 0.5).astype(I32) * (1 << k)
                left[i] = left[i] | lax.shift_left(bits, base)
    for u, (dy, dz) in enumerate(B_PLACES):
        base = ((yh + dy) % YH * NZ + (z + dz) % NZ) * cols
        plan_ref[PLAN_B + u] = base
        if u in B_LATE:
            late = late | lax.shift_left(jnp.int32(whole), base)
    plan_ref[PLAN_LATE] = late
    for j in range(NC * cols):
        m = jnp.int32(0)
        for q in range(parts):
            for i in range(cols):
                at = j % cols * grid + (q * NC + c) * cols + i
                flag = right_ref[at] if j < cols else other_ref[at]
                m = m + (flag > 0.5).astype(I32) * (1 << (q * cols + i))
        plan_ref[PLAN_RIGHT + j] = m
    for i in range(rows):
        for j in range(NC * cols):
            flag = out_ref[j * rows + i] if j < cols else other_ref[n_right + (j - cols) * rows + i]
            plan_ref[PLAN_OUT + i * NC * cols + j] = (flag > 0.5).astype(I32)

    for copy in copies:
        copy.wait()
    for i in range(rows):
        m = left[i]
        for u in range(len(units)):
            bits = jnp.int32(0)
            for k in range(cols):
                full = jnp.max(corner[(u * rows + i) * cols + k].astype(F32)) > 0
                bits = bits + full.astype(I32) * (1 << k)
            m = m | lax.shift_left(bits, bases[u])
        plan_ref[PLAN_LEFT + i] = m


def planned(rows, cols, far, right, keep_out, other, units):
    count = len(units) * rows * cols
    return pl.pallas_call(
        functools.partial(plan_kernel, rows, cols),
        out_shape=jax.ShapeDtypeStruct((PLAN_SIZE,), I32),
        in_specs=[SMEM] * 4 + [ANY] * len(units),
        out_specs=SMEM,
        scratch_shapes=[pltpu.VMEM((count, 16, 128), BF16), pltpu.SemaphoreType.DMA((count,))],
        compiler_params=vmem_limit(4),
        cost_estimate=pl.CostEstimate(flops=10**6, bytes_accessed=2**10, transcendentals=0),
        name="plan",
    )(far, right, keep_out, other, *units)


def product_kernel(n_a, n_b, shape, cols_out, begun, *refs):
    rows, cols, grid, tile = shape
    plan, refs = refs[0], refs[1:]
    refs = refs[begun:]
    a_in, b_in, refs = refs[:n_a], refs[n_a:n_a + n_b], refs[n_a + n_b:]
    n_out = 1 if begun else 2
    out_refs, (a_buf, b_buf, order, a_sem, b_sem) = refs[:n_out], refs[n_out:]
    wide = len(cols_out)
    no_a, no_b = rows * grid, wide * grid
    deep = a_in[0].shape[1] // tile

    when = plan[PLAN_LATE] if begun else ~plan[PLAN_LATE]
    used = {}
    for i in range(rows):
        for j in cols_out:
            pair = plan[PLAN_LEFT + i] & plan[PLAN_RIGHT + j] & when
            used[i, j] = jnp.where(plan[PLAN_OUT + i * cols + j] > 0, pair, 0)
    need_a = [functools.reduce(jnp.bitwise_or, [used[i, j] for j in cols_out]) for i in range(rows)]
    need_b = [functools.reduce(jnp.bitwise_or, [used[i, j] for i in range(rows)]) for j in cols_out]

    def tile_at(ref, i, j):
        return ref.at[pl.ds(i * tile, tile), pl.ds(j * tile, tile)]

    def each(act):
        for u in range(n_a):
            base = plan[PLAN_A + u]
            bits = [lax.shift_right_logical(m, base) & ((1 << deep) - 1) for m in need_a]

            @pl.when(functools.reduce(jnp.bitwise_or, bits) > 0)
            def _(u=u, base=base, bits=bits):
                for i in range(rows):
                    for k in range(deep):
                        @pl.when(bits[i] & (1 << k) > 0)
                        def _(i=i, k=k):
                            slot = i * grid + base + k
                            act(pltpu.make_async_copy(tile_at(a_in[u], i, k), a_buf.at[slot], a_sem.at[slot]))
        for u in range(n_b):
            base = plan[PLAN_B + u]
            bits = [lax.shift_right_logical(m, base) & ((1 << deep) - 1) for m in need_b]

            @pl.when(functools.reduce(jnp.bitwise_or, bits) > 0)
            def _(u=u, base=base, bits=bits):
                for n, j in enumerate(cols_out):
                    for k in range(deep):
                        @pl.when(bits[n] & (1 << k) > 0)
                        def _(n=n, j=j, k=k):
                            slot = n * grid + base + k
                            act(pltpu.make_async_copy(tile_at(b_in[u], k, j), b_buf.at[slot], b_sem.at[slot]))

    each(lambda copy: copy.start())
    a_buf[no_a] = jnp.zeros((tile, tile), BF16)
    b_buf[no_b] = jnp.zeros((tile, tile), BF16)
    count = {}
    for n, j in enumerate(cols_out):
        for i in range(rows):
            first = (n * rows + i) * (grid + GROUP)
            at = jnp.int32(first)
            for k in range(grid):
                order[at] = k
                at = at + (lax.shift_right_logical(used[i, j], k) & 1)
            for g in range(GROUP - 1):
                order[at + g] = grid
            count[i, j] = (at - first + GROUP - 1) // GROUP
    each(lambda copy: copy.wait())

    for n, j in enumerate(cols_out):
        out_ref = out_refs[n * n_out // wide]
        place = n % (wide // n_out)
        for i in range(rows):
            here = slice(i * tile, (i + 1) * tile), slice(place * tile, (place + 1) * tile)
            if not begun:
                out_ref[here] = jnp.zeros((tile, tile), F32)

            def step(m, _, i=i, n=n, here=here, out_ref=out_ref):
                part = None
                for g in range(GROUP):
                    k = order[(n * rows + i) * (grid + GROUP) + m * GROUP + g]
                    a_tile = a_buf[jnp.where(k < grid, i * grid + k, no_a)]
                    b_tile = b_buf[jnp.where(k < grid, n * grid + k, no_b)]
                    dot = jnp.dot(a_tile, b_tile, preferred_element_type=F32)
                    part = dot if part is None else part + dot
                out_ref[here] += part
                return 0

            lax.fori_loop(0, count[i, j], step, 0)


def product(plan, a_units, b_units, rows, cols, cols_out, start=None):
    begun = start is not None
    tile = a_units[0].shape[0] // rows
    grid = YL * NX * (a_units[0].shape[1] // tile)
    half = jax.ShapeDtypeStruct((rows * tile, cols // NC * tile), F32)
    n_out = 1 if begun else NC
    return pl.pallas_call(
        functools.partial(product_kernel, len(a_units), len(b_units), (rows, cols, grid, tile), cols_out, begun),
        out_shape=(half,) * n_out,
        in_specs=[SMEM] + [VMEM] * begun + [ANY] * (len(a_units) + len(b_units)),
        out_specs=(VMEM,) * n_out,
        scratch_shapes=[
            pltpu.VMEM((rows * grid + 1, tile, tile), BF16),
            pltpu.VMEM((len(cols_out) * grid + 1, tile, tile), BF16),
            pltpu.SMEM((rows * len(cols_out) * (grid + GROUP),), I32),
            pltpu.SemaphoreType.DMA((rows * grid,)),
            pltpu.SemaphoreType.DMA((len(cols_out) * grid,)),
        ],
        compiler_params=vmem_limit(26),
        cost_estimate=pl.CostEstimate(flops=10**6, bytes_accessed=2**10, transcendentals=0),
        input_output_aliases={1: 0} if begun else {},
        name="finish" if begun else "begin",
    )(plan, *([start] if begun else []), *a_units, *b_units)


def shards(entries, pattern, prune):
    col = lax.axis_index("col")
    rows, cols = pattern.shape
    height, width = entries.shape
    grid = rows * lax.axis_size("row")
    c = col % NC

    masked, message, flags = mask(pattern, entries)
    flags = flags[0, :rows * cols]
    row_ids = lax.axis_index("row") * rows + jnp.arange(rows, dtype=I32)
    col_ids = col * cols + jnp.arange(cols, dtype=I32)
    diagonal = (col_ids[:, None] == row_ids[None, :]).astype(I32)
    kept = jnp.maximum(prune.T, diagonal).astype(F32).reshape(-1)

    flags = jnp.concatenate([flags, move(flags, SWAP_CORE)])
    message = row_sum(message, flags)
    colsum, right = message[:, :width], message[0, width:width + grid * cols]
    a = (masked / colsum).astype(BF16)

    half = height // 2
    mine = lax.dynamic_slice(a, (c * half, 0), (half, width))
    theirs = lax.dynamic_slice(a, ((1 - c) * half, 0), (half, width))
    b = jnp.concatenate([mine, move(theirs, SWAP_CORE)], axis=1)

    flags = after(flags, a)
    far = jnp.concatenate([move(flags, far) for far in FAR_1])
    a, far = lax.optimization_barrier((a, far))
    notes_o = move(jnp.concatenate([right, kept, far]), SWAP_CORE)

    xl, xr, pa = move(a, X_UP), move(a, X_DOWN), move(a, SWAP_YL)
    zl, zr = move(after(b, far), Z_UP), move(b, Z_DOWN)
    pxl, pxr = move(after(pa, xl), X_UP), move(after(pa, xr, zl, zr), X_DOWN)
    zf, pb = move(after(zl, zr), Z_UP), move(after(b, pa, xl), SWAP_YH)
    xf, pxf = move(after(xl, pxl), X_UP), move(pxr, X_DOWN)
    pzl, pzr, pzf = move(after(pb, zf), Z_UP), move(pb, Z_DOWN), move(after(zf, pb), SWAP_YH)
    notes_o, far, right = after(notes_o, pxl, pxr, pb), after(far, pxl, pxr, pb), after(right, pxl, pxr, pb)

    a_units = [a, xl, xr, pa, pxl, pxr, xf, pxf]
    plan = planned(rows, cols, far, right, kept, notes_o, a_units[:6])
    b_units = [b, zl, zr, zf, pb, pzl, pzr, pzf]
    wide = NC * cols
    mine, theirs = product(plan, a_units[:6], b_units[:5], rows, wide, tuple(range(wide)))
    theirs, = product(plan, a_units, b_units, rows, wide, tuple(range(cols, wide)), theirs)
    got = move(theirs, SWAP_CORE)
    mine, = product(plan, a_units, b_units, rows, wide, tuple(range(cols)), mine)
    inflated, total = squared(mine, got)
    total = row_sum(total)
    return rescaled(float(height * lax.axis_size("row")), inflated, total)


def solution(mesh):
    return jax.shard_map(
        shards,
        mesh=mesh,
        in_specs=(P("row", "col"), P("row", "col"), P("row", "col")),
        out_specs=P("row", "col"),
        check_vma=False,
    )
```

```python
import functools
import jax
import jax.numpy as jnp
from jax import lax
from jax.experimental import pallas as pl
from jax.experimental.pallas import tpu as pltpu
from jax.sharding import PartitionSpec as P

AXES = ("row", "col")
YH, NZ, YL, NX, NC = 2, 4, 2, 4, 2
F32 = jnp.float32
BF16 = jnp.bfloat16
I32 = jnp.int32
GROUP = 4


def place(yh, z, yl, x, c):
    return (yh * NZ + z) * (YL * NX * NC) + (yl * NX + x) * NC + c


def pairs(step, cores=range(NC)):
    return [
        (place(yh, z, yl, x, c), place(*step(yh, z, yl, x, c)))
        for yh in range(YH)
        for z in range(NZ)
        for yl in range(YL)
        for x in range(NX)
        for c in cores
    ]


X_UP = pairs(lambda yh, z, yl, x, c: (yh, z, yl, (x + 1) % NX, c))
X_DOWN = pairs(lambda yh, z, yl, x, c: (yh, z, yl, (x - 1) % NX, c))
Z_UP = pairs(lambda yh, z, yl, x, c: (yh, (z + 1) % NZ, yl, x, c))
Z_DOWN = pairs(lambda yh, z, yl, x, c: (yh, (z - 1) % NZ, yl, x, c))
SWAP_CORE = pairs(lambda yh, z, yl, x, c: (yh, z, yl, x, 1 - c))
SWAP_YL = pairs(lambda yh, z, yl, x, c: (yh, z, 1 - yl, x, c))
SWAP_YH = pairs(lambda yh, z, yl, x, c: (1 - yh, z, yl, x, c))
FAR_1 = [
    pairs(lambda yh, z, yl, x, c, dy=dy: (yh, z, (yl + dy) % YL, (x + 2) % NX, c), cores=(1,))
    for dy in (0, 1)
]
Z_TURNS = [pairs(lambda yh, z, yl, x, c, d=d: (yh, (z + d) % NZ, yl, x, c)) for d in (1, 3, 2)]


def move(value, perm):
    return lax.ppermute(value, AXES, perm)


def turn_sum(value, turns):
    return value + sum(move(value, turn) for turn in turns)


def row_sum(value, *beside):
    value = turn_sum(value, Z_TURNS)
    if beside:
        value = after(value, *beside)
    return value + move(value, SWAP_YH)


def after(value, *deps):
    return lax.optimization_barrier((value, *deps))[0]


def vmem_limit(mib):
    return pltpu.CompilerParams(vmem_limit_bytes=mib * 2**20)


VMEM = pl.BlockSpec(memory_space=pltpu.VMEM)
SMEM = pl.BlockSpec(memory_space=pltpu.SMEM)
ANY = pl.BlockSpec(memory_space=pl.ANY)


LANES = 128


def mask_kernel(pattern_in, entries_in, masked_ref, message_ref, flags_ref, pattern_ref, entries_ref, sem):
    cols, rows = pattern_ref.shape
    tall, wide = entries_ref.shape[0] // rows, entries_ref.shape[1] // cols
    small = pltpu.make_async_copy(pattern_in, pattern_ref, sem.at[rows])
    strips = [
        pltpu.make_async_copy(
            entries_in.at[pl.ds(i * tall, tall)], entries_ref.at[pl.ds(i * tall, tall)], sem.at[i]
        )
        for i in range(rows)
    ]
    for copy in [small] + strips:
        copy.start()
    row, col = lax.axis_index("row"), lax.axis_index("col")
    grid = lax.axis_size("row") * rows
    lane = lax.broadcasted_iota(I32, (1, LANES), 1)
    column_flags = jnp.zeros((1, LANES), F32)
    flags = jnp.zeros((1, LANES), F32)
    totals = [jnp.zeros((1, wide), F32) for _ in range(cols)]
    small.wait()
    for i in range(rows):
        strips[i].wait()
        down = slice(i * tall, (i + 1) * tall)
        for j in range(cols):
            right = slice(j * wide, (j + 1) * wide)
            diagonal = (row * rows + i == col * cols + j).astype(I32)
            keep = jnp.maximum(pattern_ref[j, i], diagonal).astype(F32)
            masked = entries_ref[down, right] * keep
            masked_ref[down, right] = masked
            totals[j] = totals[j] + jnp.sum(masked, axis=0, keepdims=True)
            column_flags = jnp.where(lane == j * grid + row * rows + i, keep, column_flags)
            flags = jnp.where(lane == j * rows + i, keep, flags)
    for j in range(cols):
        message_ref[:, j * wide:(j + 1) * wide] = totals[j]
    message_ref[:, cols * wide:] = column_flags
    flags_ref[...] = flags


def mask(pattern, entries):
    return pl.pallas_call(
        mask_kernel,
        out_shape=(
            jax.ShapeDtypeStruct(entries.shape, F32),
            jax.ShapeDtypeStruct((1, entries.shape[1] + LANES), F32),
            jax.ShapeDtypeStruct((1, LANES), F32),
        ),
        in_specs=[ANY] * 2,
        out_specs=(VMEM, VMEM, VMEM),
        scratch_shapes=[
            pltpu.SMEM(pattern.shape[::-1], I32),
            pltpu.VMEM(entries.shape, F32),
            pltpu.SemaphoreType.DMA((pattern.shape[0] + 1,)),
        ],
        compiler_params=vmem_limit(16),
        name="mask",
    )(pattern.T, entries)


def square_kernel(mine_ref, got_ref, out_ref, sum_ref):
    rows = out_ref.shape[0]
    step = rows // 4
    total = jnp.zeros(sum_ref.shape, F32)
    for r in range(0, rows, step):
        full = mine_ref[r:r + step, :] + got_ref[r:r + step, :]
        square = full * full
        out_ref[r:r + step, :] = square
        total = total + jnp.sum(square, axis=0, keepdims=True)
    sum_ref[...] = total


def squared(mine, got):
    return pl.pallas_call(
        square_kernel,
        out_shape=(
            jax.ShapeDtypeStruct(mine.shape, F32),
            jax.ShapeDtypeStruct((1, mine.shape[1]), F32),
        ),
        in_specs=[VMEM, VMEM],
        out_specs=(VMEM, VMEM),
        compiler_params=vmem_limit(16),
        name="square",
    )(mine, got)


def rescale_kernel(order, value_ref, total_ref, out_ref, strips, sem):
    factor = order / total_ref[...]
    n, step = strips.shape[:2]
    copies = []
    for r in range(n):
        strips[r] = value_ref[r * step:(r + 1) * step, :] * factor
        copies.append(pltpu.make_async_copy(strips.at[r], out_ref.at[pl.ds(r * step, step)], sem.at[r]))
        copies[r].start()
    for copy in copies:
        copy.wait()


def rescaled(order, value, total):
    rows, cols = value.shape
    strips = 8
    return pl.pallas_call(
        functools.partial(rescale_kernel, order),
        out_shape=jax.ShapeDtypeStruct(value.shape, F32),
        in_specs=[VMEM, VMEM],
        out_specs=ANY,
        scratch_shapes=[
            pltpu.VMEM((strips, rows // strips, cols), F32),
            pltpu.SemaphoreType.DMA((strips,)),
        ],
        compiler_params=vmem_limit(16),
        name="rescale",
    )(value, total)


PLAN_LEFT, PLAN_RIGHT, PLAN_OUT, PLAN_LATE, PLAN_A, PLAN_B, PLAN_SIZE = 0, 4, 8, 24, 25, 33, 48
A_PLACES = [(0, 0), (0, NX - 1), (0, 1), (1, 0), (1, NX - 1), (1, 1), (0, 2), (1, 2)]
B_PLACES = [(0, 0), (0, NZ - 1), (0, 1), (0, 2), (1, 0), (1, NZ - 1), (1, 1), (1, 2)]
A_LATE, B_LATE = (6, 7), (5, 6, 7)


def plan_kernel(rows, cols, far_ref, right_ref, out_ref, other_ref, *refs):
    units, (plan_ref, corner, sem) = refs[:-3], refs[-3:]
    row, col = lax.axis_index("row"), lax.axis_index("col")
    yh, z = row // NZ, row % NZ
    yl, x, c = col // (NX * NC), (col // NC) % NX, col % NC
    parts = YL * NX
    grid = parts * NC * cols
    n_right = grid * cols
    n_other = n_right + rows * cols
    tall, wide = units[0].shape[0] // rows, units[0].shape[1] // cols

    copies = []
    for u, unit in enumerate(units):
        for i in range(rows):
            for k in range(cols):
                n = (u * rows + i) * cols + k
                source = unit.at[pl.ds(i * tall, corner.shape[1]), pl.ds(k * wide, corner.shape[2])]
                copies.append(pltpu.make_async_copy(source, corner.at[n], sem.at[n]))
    for copy in copies:
        copy.start()

    late = jnp.int32(0)
    left = [jnp.int32(0)] * rows
    whole = (1 << cols) - 1
    bases = []
    for u, (dy, dx) in enumerate(A_PLACES):
        base = ((yl + dy) % YL * NX + (x + dx) % NX) * cols
        bases.append(base)
        plan_ref[PLAN_A + u] = base
        if u in A_LATE:
            late = late | lax.shift_left(jnp.int32(whole), base)
            first = (A_LATE.index(u) + len(FAR_1) - len(A_LATE)) * NC * rows * cols
            for i in range(rows):
                bits = jnp.int32(0)
                for k in range(cols):
                    if first < 0:
                        bits = jnp.int32(whole)
                    else:
                        at = first + k * rows + i
                        flag = jnp.where(c == 1, far_ref[at], other_ref[n_other + rows * cols + at])
                        bits = bits + (flag > 0.5).astype(I32) * (1 << k)
                left[i] = left[i] | lax.shift_left(bits, base)
    for u, (dy, dz) in enumerate(B_PLACES):
        base = ((yh + dy) % YH * NZ + (z + dz) % NZ) * cols
        plan_ref[PLAN_B + u] = base
        if u in B_LATE:
            late = late | lax.shift_left(jnp.int32(whole), base)
    plan_ref[PLAN_LATE] = late
    for j in range(NC * cols):
        m = jnp.int32(0)
        for q in range(parts):
            for i in range(cols):
                at = j % cols * grid + (q * NC + c) * cols + i
                flag = right_ref[at] if j < cols else other_ref[at]
                m = m + (flag > 0.5).astype(I32) * (1 << (q * cols + i))
        plan_ref[PLAN_RIGHT + j] = m
    for i in range(rows):
        for j in range(NC * cols):
            flag = out_ref[j * rows + i] if j < cols else other_ref[n_right + (j - cols) * rows + i]
            plan_ref[PLAN_OUT + i * NC * cols + j] = (flag > 0.5).astype(I32)

    for copy in copies:
        copy.wait()
    for i in range(rows):
        m = left[i]
        for u in range(len(units)):
            bits = jnp.int32(0)
            for k in range(cols):
                full = jnp.max(corner[(u * rows + i) * cols + k].astype(F32)) > 0
                bits = bits + full.astype(I32) * (1 << k)
            m = m | lax.shift_left(bits, bases[u])
        plan_ref[PLAN_LEFT + i] = m


def planned(rows, cols, far, right, keep_out, other, units):
    count = len(units) * rows * cols
    return pl.pallas_call(
        functools.partial(plan_kernel, rows, cols),
        out_shape=jax.ShapeDtypeStruct((PLAN_SIZE,), I32),
        in_specs=[SMEM] * 4 + [ANY] * len(units),
        out_specs=SMEM,
        scratch_shapes=[pltpu.VMEM((count, 16, 128), BF16), pltpu.SemaphoreType.DMA((count,))],
        compiler_params=vmem_limit(4),
        cost_estimate=pl.CostEstimate(flops=10**6, bytes_accessed=2**10, transcendentals=0),
        name="plan",
    )(far, right, keep_out, other, *units)


def product_kernel(n_a, n_b, shape, cols_out, begun, *refs):
    rows, cols, grid, tile = shape
    plan, refs = refs[0], refs[1:]
    refs = refs[begun:]
    a_in, b_in, refs = refs[:n_a], refs[n_a:n_a + n_b], refs[n_a + n_b:]
    n_out = 1 if begun else 2
    out_refs, (a_buf, b_buf, order, a_sem, b_sem) = refs[:n_out], refs[n_out:]
    wide = len(cols_out)
    no_a, no_b = rows * grid, wide * grid
    deep = a_in[0].shape[1] // tile

    when = plan[PLAN_LATE] if begun else ~plan[PLAN_LATE]
    used = {}
    for i in range(rows):
        for j in cols_out:
            pair = plan[PLAN_LEFT + i] & plan[PLAN_RIGHT + j] & when
            used[i, j] = jnp.where(plan[PLAN_OUT + i * cols + j] > 0, pair, 0)
    need_a = [functools.reduce(jnp.bitwise_or, [used[i, j] for j in cols_out]) for i in range(rows)]
    need_b = [functools.reduce(jnp.bitwise_or, [used[i, j] for i in range(rows)]) for j in cols_out]

    def tile_at(ref, i, j):
        return ref.at[pl.ds(i * tile, tile), pl.ds(j * tile, tile)]

    def each(act):
        for u in range(n_a):
            base = plan[PLAN_A + u]
            bits = [lax.shift_right_logical(m, base) & ((1 << deep) - 1) for m in need_a]

            @pl.when(functools.reduce(jnp.bitwise_or, bits) > 0)
            def _(u=u, base=base, bits=bits):
                for i in range(rows):
                    for k in range(deep):
                        @pl.when(bits[i] & (1 << k) > 0)
                        def _(i=i, k=k):
                            slot = i * grid + base + k
                            act(pltpu.make_async_copy(tile_at(a_in[u], i, k), a_buf.at[slot], a_sem.at[slot]))
        for u in range(n_b):
            base = plan[PLAN_B + u]
            bits = [lax.shift_right_logical(m, base) & ((1 << deep) - 1) for m in need_b]

            @pl.when(functools.reduce(jnp.bitwise_or, bits) > 0)
            def _(u=u, base=base, bits=bits):
                for n, j in enumerate(cols_out):
                    for k in range(deep):
                        @pl.when(bits[n] & (1 << k) > 0)
                        def _(n=n, j=j, k=k):
                            slot = n * grid + base + k
                            act(pltpu.make_async_copy(tile_at(b_in[u], k, j), b_buf.at[slot], b_sem.at[slot]))

    each(lambda copy: copy.start())
    a_buf[no_a] = jnp.zeros((tile, tile), BF16)
    b_buf[no_b] = jnp.zeros((tile, tile), BF16)
    count = {}
    for n, j in enumerate(cols_out):
        for i in range(rows):
            first = (n * rows + i) * (grid + GROUP)
            at = jnp.int32(first)
            for k in range(grid):
                order[at] = k
                at = at + (lax.shift_right_logical(used[i, j], k) & 1)
            for g in range(GROUP - 1):
                order[at + g] = grid
            count[i, j] = (at - first + GROUP - 1) // GROUP
    each(lambda copy: copy.wait())

    for n, j in enumerate(cols_out):
        out_ref = out_refs[n * n_out // wide]
        place = n % (wide // n_out)
        for i in range(rows):
            here = slice(i * tile, (i + 1) * tile), slice(place * tile, (place + 1) * tile)
            if not begun:
                out_ref[here] = jnp.zeros((tile, tile), F32)

            def step(m, _, i=i, n=n, here=here, out_ref=out_ref):
                part = None
                for g in range(GROUP):
                    k = order[(n * rows + i) * (grid + GROUP) + m * GROUP + g]
                    a_tile = a_buf[jnp.where(k < grid, i * grid + k, no_a)]
                    b_tile = b_buf[jnp.where(k < grid, n * grid + k, no_b)]
                    dot = jnp.dot(a_tile, b_tile, preferred_element_type=F32)
                    part = dot if part is None else part + dot
                out_ref[here] += part
                return 0

            lax.fori_loop(0, count[i, j], step, 0)


def product(plan, a_units, b_units, rows, cols, cols_out, start=None):
    begun = start is not None
    tile = a_units[0].shape[0] // rows
    grid = YL * NX * (a_units[0].shape[1] // tile)
    half = jax.ShapeDtypeStruct((rows * tile, cols // NC * tile), F32)
    n_out = 1 if begun else NC
    return pl.pallas_call(
        functools.partial(product_kernel, len(a_units), len(b_units), (rows, cols, grid, tile), cols_out, begun),
        out_shape=(half,) * n_out,
        in_specs=[SMEM] + [VMEM] * begun + [ANY] * (len(a_units) + len(b_units)),
        out_specs=(VMEM,) * n_out,
        scratch_shapes=[
            pltpu.VMEM((rows * grid + 1, tile, tile), BF16),
            pltpu.VMEM((len(cols_out) * grid + 1, tile, tile), BF16),
            pltpu.SMEM((rows * len(cols_out) * (grid + GROUP),), I32),
            pltpu.SemaphoreType.DMA((rows * grid,)),
            pltpu.SemaphoreType.DMA((len(cols_out) * grid,)),
        ],
        compiler_params=vmem_limit(26),
        cost_estimate=pl.CostEstimate(flops=10**6, bytes_accessed=2**10, transcendentals=0),
        input_output_aliases={1: 0} if begun else {},
        name="finish" if begun else "begin",
    )(plan, *([start] if begun else []), *a_units, *b_units)


def shards(entries, pattern, prune):
    col = lax.axis_index("col")
    rows, cols = pattern.shape
    height, width = entries.shape
    grid = rows * lax.axis_size("row")
    c = col % NC

    masked, message, flags = mask(pattern, entries)
    flags = flags[0, :rows * cols]
    row_ids = lax.axis_index("row") * rows + jnp.arange(rows, dtype=I32)
    col_ids = col * cols + jnp.arange(cols, dtype=I32)
    diagonal = (col_ids[:, None] == row_ids[None, :]).astype(I32)
    kept = jnp.maximum(prune.T, diagonal).astype(F32).reshape(-1)

    flags = jnp.concatenate([flags, move(flags, SWAP_CORE)])
    message = row_sum(message, flags)
    colsum, right = message[:, :width], message[0, width:width + grid * cols]
    a = (masked / colsum).astype(BF16)

    half = height // 2
    mine = lax.dynamic_slice(a, (c * half, 0), (half, width))
    theirs = lax.dynamic_slice(a, ((1 - c) * half, 0), (half, width))
    b = jnp.concatenate([mine, move(theirs, SWAP_CORE)], axis=1)

    flags = after(flags, a)
    far = jnp.concatenate([move(flags, far) for far in FAR_1])
    a, far = lax.optimization_barrier((a, far))
    notes_o = move(jnp.concatenate([right, kept, far]), SWAP_CORE)

    xl, xr, pa = move(a, X_UP), move(a, X_DOWN), move(a, SWAP_YL)
    zl, zr = move(after(b, far), Z_UP), move(b, Z_DOWN)
    pxl, pxr = move(after(pa, xl), X_UP), move(after(pa, xr, zl, zr), X_DOWN)
    zf, pb = move(after(zl, zr), Z_UP), move(after(b, pa, xl), SWAP_YH)
    xf, pxf = move(after(xl, pxl), X_UP), move(pxr, X_DOWN)
    pzl, pzr, pzf = move(after(pb, zf), Z_UP), move(pb, Z_DOWN), move(after(zf, pb), SWAP_YH)
    notes_o, far, right = after(notes_o, pxl, pxr, pb), after(far, pxl, pxr, pb), after(right, pxl, pxr, pb)

    a_units = [a, xl, xr, pa, pxl, pxr, xf, pxf]
    plan = planned(rows, cols, far, right, kept, notes_o, a_units[:6])
    b_units = [b, zl, zr, zf, pb, pzl, pzr, pzf]
    wide = NC * cols
    mine, theirs = product(plan, a_units[:6], b_units[:5], rows, wide, tuple(range(wide)))
    theirs, = product(plan, a_units, b_units, rows, wide, tuple(range(cols, wide)), theirs)
    got = move(theirs, SWAP_CORE)
    mine, = product(plan, a_units, b_units, rows, wide, tuple(range(cols)), mine)
    inflated, total = squared(mine, got)
    total = row_sum(total)
    return rescaled(float(height * lax.axis_size("row")), inflated, total)


def solution(mesh):
    return jax.shard_map(
        shards,
        mesh=mesh,
        in_specs=(P("row", "col"), P("row", "col"), P("row", "col")),
        out_specs=P("row", "col"),
        check_vma=False,
    )
```

```python
import functools
import jax
import jax.numpy as jnp
from jax import lax
from jax.experimental import pallas as pl
from jax.experimental.pallas import tpu as pltpu
from jax.sharding import PartitionSpec as P

AXES = ("row", "col")
YH, NZ, YL, NX, NC = 2, 4, 2, 4, 2
F32 = jnp.float32
BF16 = jnp.bfloat16
I32 = jnp.int32
GROUP = 4
PAIR = 2


def place(yh, z, yl, x, c):
    return (yh * NZ + z) * (YL * NX * NC) + (yl * NX + x) * NC + c


def pairs(step, cores=range(NC)):
    return [
        (place(yh, z, yl, x, c), place(*step(yh, z, yl, x, c)))
        for yh in range(YH)
        for z in range(NZ)
        for yl in range(YL)
        for x in range(NX)
        for c in cores
    ]


X_UP = pairs(lambda yh, z, yl, x, c: (yh, z, yl, (x + 1) % NX, c))
X_DOWN = pairs(lambda yh, z, yl, x, c: (yh, z, yl, (x - 1) % NX, c))
Z_UP = pairs(lambda yh, z, yl, x, c: (yh, (z + 1) % NZ, yl, x, c))
Z_DOWN = pairs(lambda yh, z, yl, x, c: (yh, (z - 1) % NZ, yl, x, c))
SWAP_CORE = pairs(lambda yh, z, yl, x, c: (yh, z, yl, x, 1 - c))
SWAP_YL = pairs(lambda yh, z, yl, x, c: (yh, z, 1 - yl, x, c))
SWAP_YH = pairs(lambda yh, z, yl, x, c: (1 - yh, z, yl, x, c))
FAR_1 = [
    pairs(lambda yh, z, yl, x, c, dy=dy: (yh, z, (yl + dy) % YL, (x + 2) % NX, c), cores=(1,))
    for dy in (0, 1)
]
Z_TURNS = [pairs(lambda yh, z, yl, x, c, d=d: (yh, (z + d) % NZ, yl, x, c)) for d in range(1, NZ)]


def move(value, perm):
    return lax.ppermute(value, AXES, perm)


def turn_sum(value, turns):
    return value + sum(move(value, turn) for turn in turns)


def row_sum(value, *beside):
    value = turn_sum(value, Z_TURNS)
    if beside:
        value = after(value, *beside)
    return value + move(value, SWAP_YH)


def after(value, *deps):
    return lax.optimization_barrier((value, *deps))[0]


def vmem_limit(mib):
    return pltpu.CompilerParams(vmem_limit_bytes=mib * 2**20)


VMEM = pl.BlockSpec(memory_space=pltpu.VMEM)
SMEM = pl.BlockSpec(memory_space=pltpu.SMEM)
ANY = pl.BlockSpec(memory_space=pl.ANY)


LANES = 128


def mask_kernel(pattern_in, entries_in, masked_ref, message_ref, flags_ref, pattern_ref, entries_ref, sem):
    cols, rows = pattern_ref.shape
    tall, wide = entries_ref.shape[0] // rows, entries_ref.shape[1] // cols
    small = pltpu.make_async_copy(pattern_in, pattern_ref, sem.at[rows])
    strips = [
        pltpu.make_async_copy(
            entries_in.at[pl.ds(i * tall, tall)], entries_ref.at[pl.ds(i * tall, tall)], sem.at[i]
        )
        for i in range(rows)
    ]
    for copy in [small] + strips:
        copy.start()
    row, col = lax.axis_index("row"), lax.axis_index("col")
    grid = lax.axis_size("row") * rows
    lane = lax.broadcasted_iota(I32, (1, LANES), 1)
    column_flags = jnp.zeros((1, LANES), F32)
    flags = jnp.zeros((1, LANES), F32)
    totals = [jnp.zeros((1, wide), F32) for _ in range(cols)]
    small.wait()
    for i in range(rows):
        strips[i].wait()
        down = slice(i * tall, (i + 1) * tall)
        for j in range(cols):
            right = slice(j * wide, (j + 1) * wide)
            diagonal = (row * rows + i == col * cols + j).astype(I32)
            keep = jnp.maximum(pattern_ref[j, i], diagonal).astype(F32)
            masked = entries_ref[down, right] * keep
            masked_ref[down, right] = masked
            totals[j] = totals[j] + jnp.sum(masked, axis=0, keepdims=True)
            column_flags = jnp.where(lane == j * grid + row * rows + i, keep, column_flags)
            flags = jnp.where(lane == j * rows + i, keep, flags)
    for j in range(cols):
        message_ref[:, j * wide:(j + 1) * wide] = totals[j]
    message_ref[:, cols * wide:] = column_flags
    flags_ref[...] = flags


def mask(pattern, entries):
    return pl.pallas_call(
        mask_kernel,
        out_shape=(
            jax.ShapeDtypeStruct(entries.shape, F32),
            jax.ShapeDtypeStruct((1, entries.shape[1] + LANES), F32),
            jax.ShapeDtypeStruct((1, LANES), F32),
        ),
        in_specs=[ANY] * 2,
        out_specs=(VMEM, VMEM, VMEM),
        scratch_shapes=[
            pltpu.SMEM(pattern.shape[::-1], I32),
            pltpu.VMEM(entries.shape, F32),
            pltpu.SemaphoreType.DMA((pattern.shape[0] + 1,)),
        ],
        compiler_params=vmem_limit(16),
        name="mask",
    )(pattern.T, entries)


def square_kernel(mine_ref, got_ref, out_ref, sum_ref):
    rows = out_ref.shape[0]
    step = rows // 4
    total = jnp.zeros(sum_ref.shape, F32)
    for r in range(0, rows, step):
        full = mine_ref[r:r + step, :] + got_ref[r:r + step, :]
        square = full * full
        out_ref[r:r + step, :] = square
        total = total + jnp.sum(square, axis=0, keepdims=True)
    sum_ref[...] = total


def squared(mine, got):
    return pl.pallas_call(
        square_kernel,
        out_shape=(
            jax.ShapeDtypeStruct(mine.shape, F32),
            jax.ShapeDtypeStruct((1, mine.shape[1]), F32),
        ),
        in_specs=[VMEM, VMEM],
        out_specs=(VMEM, VMEM),
        compiler_params=vmem_limit(16),
        name="square",
    )(mine, got)


def rescale_kernel(order, value_ref, total_ref, out_ref):
    factor = order / total_ref[...]
    rows = out_ref.shape[0]
    step = rows // 4
    for r in range(0, rows, step):
        out_ref[r:r + step, :] = value_ref[r:r + step, :] * factor


def rescaled(order, value, total):
    return pl.pallas_call(
        functools.partial(rescale_kernel, order),
        out_shape=jax.ShapeDtypeStruct(value.shape, F32),
        in_specs=[VMEM, VMEM],
        out_specs=VMEM,
        compiler_params=vmem_limit(16),
        name="rescale",
    )(value, total)


PLAN_LEFT, PLAN_RIGHT, PLAN_OUT, PLAN_LATE, PLAN_A, PLAN_B, PLAN_SIZE = 0, 4, 8, 24, 25, 33, 48
A_PLACES = [(0, 0), (0, NX - 1), (0, 1), (1, 0), (1, NX - 1), (1, 1), (0, 2), (1, 2)]
B_PLACES = [(0, 0), (0, NZ - 1), (0, 1), (0, 2), (1, 0), (1, NZ - 1), (1, 1), (1, 2)]
A_LATE, B_LATE = (6, 7), (5, 6, 7)


def plan_kernel(rows, cols, far_ref, right_ref, out_ref, other_ref, *refs):
    units, (plan_ref, corner, sem) = refs[:-3], refs[-3:]
    row, col = lax.axis_index("row"), lax.axis_index("col")
    yh, z = row // NZ, row % NZ
    yl, x, c = col // (NX * NC), (col // NC) % NX, col % NC
    parts = YL * NX
    grid = parts * NC * cols
    n_right = grid * cols
    n_other = n_right + rows * cols
    tall, wide = units[0].shape[0] // rows, units[0].shape[1] // cols

    copies = []
    for u, unit in enumerate(units):
        for i in range(rows):
            for k in range(cols):
                n = (u * rows + i) * cols + k
                source = unit.at[pl.ds(i * tall, corner.shape[1]), pl.ds(k * wide, corner.shape[2])]
                copies.append(pltpu.make_async_copy(source, corner.at[n], sem.at[n]))
    for copy in copies:
        copy.start()

    late = jnp.int32(0)
    left = [jnp.int32(0)] * rows
    whole = (1 << cols) - 1
    bases = []
    for u, (dy, dx) in enumerate(A_PLACES):
        base = ((yl + dy) % YL * NX + (x + dx) % NX) * cols
        bases.append(base)
        plan_ref[PLAN_A + u] = base
        if u in A_LATE:
            late = late | lax.shift_left(jnp.int32(whole), base)
            first = (A_LATE.index(u) + len(FAR_1) - len(A_LATE)) * NC * rows * cols
            for i in range(rows):
                bits = jnp.int32(0)
                for k in range(cols):
                    if first < 0:
                        bits = jnp.int32(whole)
                    else:
                        at = first + k * rows + i
                        flag = jnp.where(c == 1, far_ref[at], other_ref[n_other + rows * cols + at])
                        bits = bits + (flag > 0.5).astype(I32) * (1 << k)
                left[i] = left[i] | lax.shift_left(bits, base)
    for u, (dy, dz) in enumerate(B_PLACES):
        base = ((yh + dy) % YH * NZ + (z + dz) % NZ) * cols
        plan_ref[PLAN_B + u] = base
        if u in B_LATE:
            late = late | lax.shift_left(jnp.int32(whole), base)
    plan_ref[PLAN_LATE] = late
    for j in range(NC * cols):
        m = jnp.int32(0)
        for q in range(parts):
            for i in range(cols):
                at = j % cols * grid + (q * NC + c) * cols + i
                flag = right_ref[at] if j < cols else other_ref[at]
                m = m + (flag > 0.5).astype(I32) * (1 << (q * cols + i))
        plan_ref[PLAN_RIGHT + j] = m
    for i in range(rows):
        for j in range(NC * cols):
            flag = out_ref[j * rows + i] if j < cols else other_ref[n_right + (j - cols) * rows + i]
            plan_ref[PLAN_OUT + i * NC * cols + j] = (flag > 0.5).astype(I32)

    for copy in copies:
        copy.wait()
    for i in range(rows):
        m = left[i]
        for u in range(len(units)):
            bits = jnp.int32(0)
            for k in range(cols):
                full = jnp.max(corner[(u * rows + i) * cols + k].astype(F32)) > 0
                bits = bits + full.astype(I32) * (1 << k)
            m = m | lax.shift_left(bits, bases[u])
        plan_ref[PLAN_LEFT + i] = m


def planned(rows, cols, far, right, keep_out, other, units):
    count = len(units) * rows * cols
    return pl.pallas_call(
        functools.partial(plan_kernel, rows, cols),
        out_shape=jax.ShapeDtypeStruct((PLAN_SIZE,), I32),
        in_specs=[SMEM] * 4 + [ANY] * len(units),
        out_specs=SMEM,
        scratch_shapes=[pltpu.VMEM((count, 16, 128), BF16), pltpu.SemaphoreType.DMA((count,))],
        compiler_params=vmem_limit(4),
        cost_estimate=pl.CostEstimate(flops=10**6, bytes_accessed=2**10, transcendentals=0),
        name="plan",
    )(far, right, keep_out, other, *units)


def product_kernel(n_a, n_b, shape, cols_out, begun, *refs):
    rows, cols, grid, tile = shape
    plan, refs = refs[0], refs[1:]
    refs = refs[begun:]
    a_in, b_in, refs = refs[:n_a], refs[n_a:n_a + n_b], refs[n_a + n_b:]
    n_out = 1 if begun else 2
    out_refs, (a_buf, b_buf, order, a_sem, b_sem) = refs[:n_out], refs[n_out:]
    wide = len(cols_out)
    no_a, no_b = rows * grid, wide * grid
    deep = a_in[0].shape[1] // tile

    when = plan[PLAN_LATE] if begun else ~plan[PLAN_LATE]
    used = {}
    for i in range(rows):
        for j in cols_out:
            pair = plan[PLAN_LEFT + i] & plan[PLAN_RIGHT + j] & when
            used[i, j] = jnp.where(plan[PLAN_OUT + i * cols + j] > 0, pair, 0)
    need_a = [functools.reduce(jnp.bitwise_or, [used[i, j] for j in cols_out]) for i in range(rows)]
    need_b = [functools.reduce(jnp.bitwise_or, [used[i, j] for i in range(rows)]) for j in cols_out]

    def tile_at(ref, i, j):
        return ref.at[pl.ds(i * tile, tile), pl.ds(j * tile, tile)]

    def each(act):
        for u in range(n_a):
            base = plan[PLAN_A + u]
            bits = [lax.shift_right_logical(m, base) & ((1 << deep) - 1) for m in need_a]

            @pl.when(functools.reduce(jnp.bitwise_or, bits) > 0)
            def _(u=u, base=base, bits=bits):
                for i in range(rows):
                    for k in range(deep):
                        @pl.when(bits[i] & (1 << k) > 0)
                        def _(i=i, k=k):
                            slot = i * grid + base + k
                            act(pltpu.make_async_copy(tile_at(a_in[u], i, k), a_buf.at[slot], a_sem.at[slot]))
        for u in range(n_b):
            base = plan[PLAN_B + u]
            bits = [lax.shift_right_logical(m, base) & ((1 << deep) - 1) for m in need_b]

            @pl.when(functools.reduce(jnp.bitwise_or, bits) > 0)
            def _(u=u, base=base, bits=bits):
                for n, j in enumerate(cols_out):
                    for k in range(deep):
                        @pl.when(bits[n] & (1 << k) > 0)
                        def _(n=n, j=j, k=k):
                            slot = n * grid + base + k
                            act(pltpu.make_async_copy(tile_at(b_in[u], k, j), b_buf.at[slot], b_sem.at[slot]))

    each(lambda copy: copy.start())
    a_buf[no_a] = jnp.zeros((tile, tile), BF16)
    b_buf[no_b] = jnp.zeros((tile, tile), BF16)
    count = {}
    for n, j in enumerate(cols_out):
        for i in range(rows):
            first = (n * rows + i) * (grid + GROUP)
            at = jnp.int32(first)
            for k in range(grid):
                order[first + k] = grid
            for k in range(grid):
                order[at] = k
                at = at + (lax.shift_right_logical(used[i, j], k) & 1)
            order[at] = grid
            count[i, j] = (at - first + GROUP - 1) // GROUP
    each(lambda copy: copy.wait())

    for n in range(0, wide, PAIR):
        for i in range(rows):
            outs = []
            for p in range(PAIR):
                place = (n + p) % (wide // n_out)
                here = slice(i * tile, (i + 1) * tile), slice(place * tile, (place + 1) * tile)
                outs.append((out_refs[(n + p) * n_out // wide], here))
            if not begun:
                for out_ref, here in outs:
                    out_ref[here] = jnp.zeros((tile, tile), F32)

            def step(m, _, i=i, n=n, outs=outs):
                for p, (out_ref, here) in enumerate(outs):
                    part = None
                    for g in range(GROUP):
                        k = order[((n + p) * rows + i) * (grid + GROUP) + m * GROUP + g]
                        a_tile = a_buf[jnp.where(k < grid, i * grid + k, no_a)]
                        b_tile = b_buf[jnp.where(k < grid, (n + p) * grid + k, no_b)]
                        dot = jnp.dot(a_tile, b_tile, preferred_element_type=F32)
                        part = dot if part is None else part + dot
                    out_ref[here] += part
                return 0

            steps = [count[i, cols_out[n + p]] for p in range(PAIR)]
            lax.fori_loop(0, functools.reduce(jnp.maximum, steps), step, 0)


def product(plan, a_units, b_units, rows, cols, cols_out, start=None):
    begun = start is not None
    tile = a_units[0].shape[0] // rows
    grid = YL * NX * (a_units[0].shape[1] // tile)
    half = jax.ShapeDtypeStruct((rows * tile, cols // NC * tile), F32)
    n_out = 1 if begun else NC
    return pl.pallas_call(
        functools.partial(product_kernel, len(a_units), len(b_units), (rows, cols, grid, tile), cols_out, begun),
        out_shape=(half,) * n_out,
        in_specs=[SMEM] + [VMEM] * begun + [ANY] * (len(a_units) + len(b_units)),
        out_specs=(VMEM,) * n_out,
        scratch_shapes=[
            pltpu.VMEM((rows * grid + 1, tile, tile), BF16),
            pltpu.VMEM((len(cols_out) * grid + 1, tile, tile), BF16),
            pltpu.SMEM((rows * len(cols_out) * (grid + GROUP),), I32),
            pltpu.SemaphoreType.DMA((rows * grid,)),
            pltpu.SemaphoreType.DMA((len(cols_out) * grid,)),
        ],
        compiler_params=vmem_limit(26),
        cost_estimate=pl.CostEstimate(flops=10**6, bytes_accessed=2**10, transcendentals=0),
        input_output_aliases={1: 0} if begun else {},
        name="finish" if begun else "begin",
    )(plan, *([start] if begun else []), *a_units, *b_units)


def shards(entries, pattern, prune):
    col = lax.axis_index("col")
    rows, cols = pattern.shape
    height, width = entries.shape
    grid = rows * lax.axis_size("row")
    c = col % NC

    masked, message, flags = mask(pattern, entries)
    flags = flags[0, :rows * cols]
    row_ids = lax.axis_index("row") * rows + jnp.arange(rows, dtype=I32)
    col_ids = col * cols + jnp.arange(cols, dtype=I32)
    diagonal = (col_ids[:, None] == row_ids[None, :]).astype(I32)
    kept = jnp.maximum(prune.T, diagonal).astype(F32).reshape(-1)

    flags = jnp.concatenate([flags, move(flags, SWAP_CORE)])
    message = row_sum(message, flags)
    colsum, right = message[:, :width], message[0, width:width + grid * cols]
    a = (masked / colsum).astype(BF16)

    half = height // 2
    mine = lax.dynamic_slice(a, (c * half, 0), (half, width))
    theirs = lax.dynamic_slice(a, ((1 - c) * half, 0), (half, width))
    b = jnp.concatenate([mine, move(theirs, SWAP_CORE)], axis=1)

    flags = after(flags, a)
    far = jnp.concatenate([move(flags, far) for far in FAR_1])
    a, far = lax.optimization_barrier((a, far))
    notes_o = move(jnp.concatenate([right, kept, far]), SWAP_CORE)

    xl, xr, pa = move(a, X_UP), move(a, X_DOWN), move(a, SWAP_YL)
    zl, zr = move(after(b, far), Z_UP), move(b, Z_DOWN)
    pxl, pxr = move(after(pa, xl), X_UP), move(after(pa, xr, zl, zr), X_DOWN)
    zf, pb = move(after(zl, zr), Z_UP), move(after(b, pa, xl), SWAP_YH)
    xf, pxf = move(after(xl, pxl), X_UP), move(pxr, X_DOWN)
    pzl, pzr, pzf = move(after(pb, zf), Z_UP), move(pb, Z_DOWN), move(after(zf, pb), SWAP_YH)
    notes_o, far, right = after(notes_o, pxl, pxr, pb), after(far, pxl, pxr, pb), after(right, pxl, pxr, pb)

    a_units = [a, xl, xr, pa, pxl, pxr, xf, pxf]
    plan = planned(rows, cols, far, right, kept, notes_o, a_units[:6])
    b_units = [b, zl, zr, zf, pb, pzl, pzr, pzf]
    wide = NC * cols
    mine, theirs = product(plan, a_units[:6], b_units[:5], rows, wide, tuple(range(wide)))
    theirs, = product(plan, a_units, b_units, rows, wide, tuple(range(cols, wide)), theirs)
    got = move(theirs, SWAP_CORE)
    mine, = product(plan, a_units, b_units, rows, wide, tuple(range(cols)), mine)
    inflated, total = squared(mine, got)
    total = row_sum(total)
    return rescaled(float(height * lax.axis_size("row")), inflated, total)


def solution(mesh):
    return jax.shard_map(
        shards,
        mesh=mesh,
        in_specs=(P("row", "col"), P("row", "col"), P("row", "col")),
        out_specs=P("row", "col"),
        check_vma=False,
    )
```
